32 devices in a mesh: segment: 4 (over y, x), gz: 8 (over z, core).
Axes of the slice: x: 2, y: 2, z: 4, core: 2. Of those that a mesh axis runs over, the one named last changes fastest.
Arguments:
- start_volume: float32 [4, 128, 1024], P(None, 'gz'), may hold values from -6 to 6
- sinogram: float32 [4, 128, 1024], P(None, 'gz'), may hold values from -6 to 6
- offsets: int32 [4, 8], replicated, may hold values from -15 to 15, as said below
- projector: bfloat16 [3, 1024, 1024], replicated, may hold values from -0.109375 to 0.109375
- dual_in: bfloat16 [32, 27], replicated, may hold values from -1.25 to 1.25
- dual_out: bfloat16 [9, 32], replicated, may hold values from -0.375 to 0.375
- primal_in: bfloat16 [64, 54], replicated, may hold values from -0.875 to 0.875
- primal_out: bfloat16 [27, 64], replicated, may hold values from -0.15625 to 0.15625
Outputs:
- volume: float32 [4, 128, 1024], P('segment', 'gz')
The draws below stay inside these ranges and needn't reach their ends.
Inputs may be any that keep to these rules, and one draw needn't show every extreme that they name: `offsets`: both ends of the range are taken in every draw.
All inputs are finite; a program needn't handle non-finite values.
Results may differ from the reference program's by a relative error of at most 0.005.
Values may be sent and summed in bfloat16 or wider, within the bound.
No kernel may reach another device: no remote copies, remote signals or barrier semaphores. Data moves between devices by JAX's collectives and lax.ppermute only.
A program may use at most 64 MiB of HBM per device.

```python
import jax
import jax.numpy as jnp
from jax import lax

ZL = 16
IMG = 32
NCOL = 128
VIEWS = 8
DUAL_CH = 32
PRIMAL_CH = 64
ITERS = 2
SLABS = 4
Z = 128
CELLS = 1024


def draw_offsets(key, part):
    key_values = jax.random.fold_in(key, 11)
    key_places = jax.random.fold_in(key, 23)
    drawn = jax.random.randint(key_values, (SLABS * VIEWS,), -(ZL - 1), ZL, dtype=jnp.int32)
    order = jax.random.permutation(key_places, SLABS * VIEWS)
    drawn = drawn.at[order[0]].set(ZL - 1)
    drawn = drawn.at[order[1]].set(-(ZL - 1))
    return drawn.reshape(SLABS, VIEWS)


def steps_of(own_key, shape, cuts, low, largest):
    factor_of = 1.0
    for position, shards_of in cuts:
        heights = jax.random.uniform(jax.random.fold_in(jax.random.fold_in(own_key, 6), position), (shards_of,), jnp.float32, low / len(cuts), largest / len(cuts))
        factor_of = factor_of * jnp.repeat(jnp.exp(heights), shape[position] // shards_of).reshape((-1,) + (1,) * (len(shape) - 1 - position))
    return factor_of


def normal_values(stream_key, extent, width, limit, cuts=(), held_as=jnp.bfloat16):
    values = jax.random.normal(stream_key, extent, jnp.float32) * width
    if len(cuts) > 0:
        values = steps_of(stream_key, extent, cuts, -0.22, 0.18) * values
    return jnp.clip(values, min=-limit, max=limit).astype(held_as)


def setup_inputs(seed: int = 0) -> dict:
    seeds = jax.random.split(jax.random.key(seed), 9)
    return {
        "start_volume": normal_values(seeds[0], (SLABS, Z, CELLS), 1.0, 6.0, ((1, 8),), jnp.float32),
        "sinogram": normal_values(seeds[1], (SLABS, Z, CELLS), 1.0, 6.0, ((1, 8),), jnp.float32),
        "offsets": draw_offsets(jax.random.fold_in(seeds[8], 71), 0),
        "projector": normal_values(seeds[3], (3, CELLS, CELLS), (3 * CELLS) ** -0.5, 0.109375),
        "dual_in": normal_values(seeds[4], (DUAL_CH, 27), 27 ** -0.5, 1.25),
        "dual_out": normal_values(seeds[5], (9, DUAL_CH), (9 * DUAL_CH) ** -0.5, 0.375),
        "primal_in": normal_values(seeds[6], (PRIMAL_CH, 54), 54 ** -0.5, 0.875),
        "primal_out": normal_values(seeds[7], (27, PRIMAL_CH), (27 * PRIMAL_CH) ** -0.5, 0.15625),
    }


def plane_taps(flavour):
    cell_count = IMG * IMG
    positions = jnp.arange(cell_count, dtype=jnp.int32)
    tap_list = []
    if flavour == 0:
        column_of = positions % NCOL
        for step_size in (-1, 0, 1):
            keep_mask = ((column_of + step_size >= 0) & (column_of + step_size < NCOL)).astype(jnp.float32)
            tap_list.append((step_size, keep_mask))
    else:
        row_of = positions // IMG
        column_of = positions % IMG
        for down_step in (-1, 0, 1):
            for across_step in (-1, 0, 1):
                keep_mask = ((row_of + down_step >= 0) & (row_of + down_step < IMG) & (column_of + across_step >= 0) & (column_of + across_step < IMG)).astype(jnp.float32)
                tap_list.append((down_step * IMG + across_step, keep_mask))
    return tap_list


def plane_shift(values, offset, keep_mask):
    margin = IMG + 1
    cell_count = values.shape[-1]
    widths = [(0, 0)] * (values.ndim - 1) + [(margin, margin)]
    padded = jnp.pad(values, widths)
    shifted = lax.slice_in_dim(padded, margin + offset, margin + offset + cell_count, axis=values.ndim - 1)
    return shifted * keep_mask.astype(values.dtype)


def expand(source, row_count, tap_list):
    pieces = []
    for depth_index in range(3):
        layer_rows = lax.slice_in_dim(source, depth_index, depth_index + row_count, axis=1)
        for offset, keep_mask in tap_list:
            pieces.append(plane_shift(layer_rows, offset, keep_mask))
    return jnp.concatenate(pieces, axis=0)


def collapse(hidden, w_second, row_count, tap_list):
    partial_value = jnp.einsum("to,ozn->tzn", w_second, hidden)
    summed = jnp.zeros((row_count, hidden.shape[2]), jnp.float32)
    tap_number = 0
    for depth_index in range(3):
        for offset, keep_mask in tap_list:
            layer_rows = lax.slice_in_dim(partial_value[tap_number], depth_index, depth_index + row_count, axis=0)
            summed = summed + plane_shift(layer_rows, offset, keep_mask)
            tap_number = tap_number + 1
    return summed


def network(channels, w_in, w_out, tap_list):
    total_rows = channels.shape[1]
    rounded = lax.optimization_barrier(channels.astype(jnp.bfloat16)).astype(jnp.float32)
    padded = jnp.pad(rounded, ((0, 0), (2, 2), (0, 0)))
    w_first = w_in.astype(jnp.float32)
    w_second = w_out.astype(jnp.float32)

    def one_block(start_row):
        source = lax.dynamic_slice_in_dim(padded, start_row, ZL + 4, 1)
        columns = expand(source, ZL + 2, tap_list)
        hidden = jax.nn.relu(jnp.einsum("ok,kzn->ozn", w_first, columns))
        hidden = lax.optimization_barrier(hidden.astype(jnp.bfloat16)).astype(jnp.float32)
        global_row = start_row - 1 + jnp.arange(ZL + 2, dtype=jnp.int32)
        inside = ((global_row >= 0) & (global_row < total_rows)).astype(jnp.float32)
        hidden = hidden * inside[None, :, None]
        return collapse(hidden, w_second, ZL, tap_list)

    starts = jnp.arange(total_rows // ZL, dtype=jnp.int32) * ZL
    blocks = lax.map(one_block, starts)
    return blocks.reshape(total_rows, channels.shape[2])


def band_full(values, shifts, projector, adjoint):
    row_count = values.shape[0]
    cell_count = values.shape[1]
    groups = shifts.shape[0]
    group_width = cell_count // groups
    rounded = lax.optimization_barrier(values.astype(jnp.bfloat16)).astype(jnp.float32)
    padded = jnp.pad(rounded, ((ZL, ZL), (0, 0)))
    weights = projector.astype(jnp.float32)
    if adjoint:
        starts = (ZL - 1 - shifts).astype(jnp.int32)
        grouped = padded.reshape(padded.shape[0], groups, group_width)
        windows = jax.vmap(lambda column, start_row: lax.dynamic_slice_in_dim(column, start_row, row_count + 2, 0), in_axes=(1, 0))(grouped, starts)
        summed = jnp.zeros((row_count, cell_count), jnp.float32)
        for tap_row in range(3):
            window_rows = lax.slice_in_dim(windows, 2 - tap_row, 2 - tap_row + row_count, axis=1)
            summed = summed + jnp.einsum("gzc,pgc->zp", window_rows, weights[tap_row].reshape(cell_count, groups, group_width))
        return summed
    starts = (ZL - 1 + shifts).astype(jnp.int32)
    windows = jax.vmap(lambda start_row: lax.dynamic_slice_in_dim(padded, start_row, row_count + 2, 0))(starts)
    by_group = jnp.zeros((row_count, groups, group_width), jnp.float32)
    for tap_row in range(3):
        window_rows = lax.slice_in_dim(windows, tap_row, tap_row + row_count, axis=1)
        by_group = by_group + jnp.einsum("gzp,pgc->zgc", window_rows, weights[tap_row].reshape(cell_count, groups, group_width))
    return by_group.reshape(row_count, cell_count)


def reference(start_volume, sinogram, offsets, projector, dual_in, dual_out, primal_in, primal_out):
    dual_taps = plane_taps(0)
    primal_taps = plane_taps(1)
    results = []
    for slab_index in range(SLABS):
        current = start_volume[slab_index]
        dual_state = jnp.zeros_like(current)
        for rounds in range(ITERS):
            forward = band_full(current, offsets[slab_index], projector, False)
            dual_state = dual_state + network(jnp.stack([dual_state, forward, sinogram[slab_index]]), dual_in, dual_out, dual_taps)
            backward = band_full(dual_state, offsets[slab_index], projector, True)
            current = current + network(jnp.stack([current, backward]), primal_in, primal_out, primal_taps)
        results.append(current)
    return jnp.stack(results)
```

```python
import functools

import jax
import jax.numpy as jnp
import numpy as np
from jax import lax
from jax.experimental import pallas as pl
from jax.experimental.pallas import tpu as pltpu
from jax.sharding import PartitionSpec as P

IMG = 32
LANES = 128
BLOCK = 8
PAD = 16
HALO_BLOCKS = 5

DUAL_SHIFTS = (-1, 0, 1)
PRIMAL_SHIFTS = tuple((dy, dx) for dy in (-1, 0, 1) for dx in (-1, 0, 1))


def first_structure(shift_count, channels, width):
    main = shift_count * channels * BLOCK
    table = np.zeros((3 * shift_count * channels, BLOCK * width), np.float32)
    for z in range(BLOCK):
        for dz in range(3):
            row = z + dz - 1
            for s in range(shift_count):
                for c in range(channels):
                    if row < 0:
                        column = main + s * BLOCK + 2 * c
                    elif row >= BLOCK:
                        column = main + s * BLOCK + 2 * c + 1
                    else:
                        column = (s * channels + c) * BLOCK + row
                    table[(dz * shift_count + s) * channels + c, z * width + column] = 1
    return table


def second_structure(shift_count, tap_width):
    table = np.zeros((shift_count * 2 * BLOCK, BLOCK * tap_width), np.float32)
    for z in range(BLOCK):
        for dz in range(3):
            row = z - dz + 1
            for s in range(shift_count):
                if row < 0:
                    place = s * 2 * BLOCK + BLOCK + BLOCK - 1
                elif row >= BLOCK:
                    place = s * 2 * BLOCK + BLOCK
                else:
                    place = s * 2 * BLOCK + row
                table[place, z * tap_width + dz * shift_count + s] = 1
    return table


def place_structure(hidden):
    return np.tile(np.eye(hidden, dtype=np.float32), (1, BLOCK))


def dot(a, b):
    return jnp.dot(a, b, preferred_element_type=jnp.float32)


def lanes():
    return lax.broadcasted_iota(jnp.int32, (BLOCK, LANES), 1)


def rows_of():
    return lax.broadcasted_iota(jnp.int32, (BLOCK, LANES), 0)


def shift_dual(tiles, step):
    if step == 0:
        return tiles
    lane = lanes()
    keep = (lane + step >= 0) & (lane + step < LANES)
    return [jnp.where(keep, pltpu.roll(t, (-step) % LANES, 1), 0.0) for t in tiles]


def shift_primal(tiles, step):
    dy, dx = step
    offset = dy * IMG + dx
    if offset == 0:
        return tiles
    lane = lanes()
    column = lane % IMG
    inside = (column + dx >= 0) & (column + dx < IMG)
    near = inside & (lane + offset >= 0) & (lane + offset < LANES)
    far = inside & ((lane + offset < 0) | (lane + offset >= LANES))
    rolled = [pltpu.roll(t, (-offset) % LANES, 1) for t in tiles]
    side = 1 if offset > 0 else -1
    out = []
    for j in range(len(tiles)):
        value = jnp.where(near, rolled[j], 0.0)
        if 0 <= j + side < len(tiles):
            value = jnp.where(far, rolled[j + side], value)
        out.append(value)
    return out


def kernel(sizes, info, own_start, *refs):
    window, tiles = sizes
    pieces = refs[:window]
    (projector, dual_in, dual_out, primal_in, primal_out, d_first, d_second, d_place,
     p_first, p_second, p_place, out, f_s, sino_s, t_s, a_s, h_s, b_s, x_s, y_s, lhs_s,
     w1d, w2d, w1p, w2p, spread) = refs[window:]
    row_count = own_start.shape[0]
    total = window * row_count
    blocks = total // BLOCK
    cells = tiles * LANES
    own = info[0]
    own_block = own // BLOCK

    def offset_of(view):
        return info[1 + window + view]

    def build(first, w_in, w1, second, place, w_out, w2, width, tap_width):
        hidden = w_in.shape[0]
        wide = dot(w_in[...], first[...])
        for z in range(BLOCK):
            w1[z * hidden:(z + 1) * hidden, :] = wide[:, z * width:(z + 1) * width].astype(jnp.bfloat16)
        across = dot(w_out[...], place[...])
        total_hidden = BLOCK * hidden
        lane = lax.broadcasted_iota(jnp.int32, across.shape, 1)
        taps = w_out.shape[0]
        spread[...] = jnp.zeros(spread.shape, spread.dtype)
        for z in range(BLOCK):
            spread[z * tap_width:z * tap_width + taps, 0:total_hidden] = jnp.where(
                lane // hidden == z, across, 0.0)
        w2[...] = dot(second[...], spread[0:BLOCK * tap_width, 0:total_hidden].astype(jnp.bfloat16)
                      ).astype(jnp.bfloat16)

    build(d_first, dual_in, w1d, d_second, d_place, dual_out, w2d, 128, 16)
    build(p_first, primal_in, w1p, p_second, p_place, primal_out, w2p, 256, 32)

    zero_rows = jnp.zeros((tiles, PAD, LANES), jnp.float32)
    for field in (f_s, sino_s, t_s, a_s):
        field[:, 0:PAD, :] = zero_rows
        field[:, PAD + total:PAD + total + PAD, :] = zero_rows
    h_s[...] = jnp.zeros(h_s.shape, jnp.float32)
    b_s[...] = jnp.zeros(b_s.shape, jnp.float32)
    x_s[...] = jnp.zeros(x_s.shape, jnp.bfloat16)
    for i, piece in enumerate(pieces):
        at = pl.multiple_of(info[1 + i] + PAD, BLOCK)
        for j in range(tiles):
            cut = slice(j * LANES, (j + 1) * LANES)
            f_s[j, pl.ds(at, row_count), :] = piece[0, :, cut].astype(jnp.float32)
            sino_s[j, pl.ds(at, row_count), :] = piece[1, :, cut].astype(jnp.float32)
    for j in range(tiles):
        f_s[j, pl.ds(pl.multiple_of(own + PAD, BLOCK), row_count), :] = own_start[:, j * LANES:(j + 1) * LANES]

    def forward(first_row, count, z_first, z_count):
        for k in range(3):
            for j in range(tiles):
                lhs_s[0:count, k * cells + j * LANES:k * cells + (j + 1) * LANES] = f_s[
                    j, pl.ds(PAD + first_row + (k - 1), count), :].astype(jnp.bfloat16)
        for n in range(cells // 256):
            value = dot(lhs_s[0:count, :], projector[:, n * 256:(n + 1) * 256])
            for part in range(2):
                t_s[2 * n + part, pl.ds(pl.multiple_of(PAD + first_row, BLOCK), count), :] = value[
                    :, part * LANES:(part + 1) * LANES]
        for w in range(tiles):
            a_s[w, pl.ds(pl.multiple_of(PAD + z_first, BLOCK), z_count), :] = t_s[
                w, pl.ds(PAD + z_first + offset_of(w), z_count), :]

    def adjoint(z_first, count):
        for k in range(3):
            for w in range(tiles):
                lhs_s[0:count, k * cells + w * LANES:k * cells + (w + 1) * LANES] = h_s[
                    w, pl.ds(PAD + z_first - offset_of(w) - (k - 1), count), :].astype(jnp.bfloat16)
        for n in range(cells // 256):
            value = jnp.zeros((count, 256), jnp.float32)
            for k in range(3):
                value = value + lax.dot_general(
                    lhs_s[0:count, k * cells:(k + 1) * cells],
                    projector[k * cells + n * 256:k * cells + (n + 1) * 256, :],
                    (((1,), (1,)), ((), ())), preferred_element_type=jnp.float32)
            for part in range(2):
                b_s[2 * n + part, pl.ds(pl.multiple_of(PAD + z_first, BLOCK), count), :] = value[
                    :, part * LANES:(part + 1) * LANES]

    def network(fields, shifts, shift_tiles, w1, w2, block_first, block_count):
        count = len(shifts)
        depth = w1.shape[1]
        edge = jnp.zeros((2 * BLOCK * count, cells), jnp.float32)
        y_s[0, 0:2 * BLOCK * count, :] = edge
        y_s[block_count + 1, 0:2 * BLOCK * count, :] = edge

        @pl.loop(0, block_count)
        def _(i):
            base = pl.multiple_of(PAD + (block_first + i) * BLOCK, BLOCK)
            row = rows_of()
            mains = [[field[j, pl.ds(base, BLOCK), :] for j in range(tiles)] for field in fields]
            edges = []
            for j in range(tiles):
                value = jnp.zeros((BLOCK, LANES), jnp.float32)
                for c, field in enumerate(fields):
                    value = jnp.where(row == 2 * c, field[j, pl.ds(base - 1 - 2 * c, BLOCK), :], value)
                    value = jnp.where(row == 2 * c + 1, field[j, pl.ds(base + BLOCK - 1 - 2 * c, BLOCK), :], value)
                edges.append(value)
            arrays = [shift_tiles(main, s) for s in shifts for main in mains]
            arrays += [shift_tiles(edges, s) for s in shifts]
            if len(arrays) % 2:
                arrays.append([jnp.zeros((BLOCK, LANES), jnp.float32)] * tiles)
            for pair in range(len(arrays) // 2):
                for j in range(tiles):
                    x_s[pair * 16:(pair + 1) * 16, j * LANES:(j + 1) * LANES] = jnp.concatenate(
                        [arrays[2 * pair][j], arrays[2 * pair + 1][j]], axis=0).astype(jnp.bfloat16)
            for n in range(cells // 256):
                hidden = dot(w1[...], x_s[0:depth, n * 256:(n + 1) * 256]).astype(jnp.bfloat16)
                hidden = jnp.maximum(hidden, jnp.zeros_like(hidden))
                y_s[i + 1, 0:2 * BLOCK * count, n * 256:(n + 1) * 256] = dot(w2[...], hidden)

    def collapse(shifts, shift_tiles, slot):
        row = rows_of()
        total_value = None
        for s, step in enumerate(shifts):
            at = s * 2 * BLOCK
            merged = []
            for j in range(tiles):
                cut = slice(j * LANES, (j + 1) * LANES)
                outer = jnp.where(row == 0, y_s[slot - 1, at + BLOCK:at + 2 * BLOCK, cut], 0.0)
                outer = jnp.where(row == BLOCK - 1, y_s[slot + 1, at + BLOCK:at + 2 * BLOCK, cut], outer)
                merged.append(y_s[slot, at:at + BLOCK, cut] + outer)
            moved = shift_tiles(merged, step)
            total_value = moved if total_value is None else [a + b for a, b in zip(total_value, moved)]
        return total_value

    def update(field, shifts, shift_tiles, block_first, block_count):
        @pl.loop(0, block_count)
        def _(i):
            base = pl.multiple_of(PAD + (block_first + i) * BLOCK, BLOCK)
            for j, value in enumerate(collapse(shifts, shift_tiles, i + 1)):
                field[j, pl.ds(base, BLOCK), :] += value

    def block_range(reach, own_count=row_count // BLOCK):
        count = min(blocks, own_count + 2 * reach)
        return jnp.clip(own_block - reach, 0, blocks - count), count

    forward(jnp.int32(-BLOCK), total + 2 * BLOCK, 0, total)
    first, count = block_range(7)
    network((h_s, a_s, sino_s), DUAL_SHIFTS, shift_dual, w1d, w2d, first, count)
    update(h_s, DUAL_SHIFTS, shift_dual, first, count)
    first, count = block_range(5)
    adjoint(first * BLOCK, count * BLOCK)
    network((f_s, b_s), PRIMAL_SHIFTS, shift_primal, w1p, w2p, first, count)
    update(f_s, PRIMAL_SHIFTS, shift_primal, first, count)

    t_count = min(total + 2 * BLOCK, row_count + 10 * BLOCK)
    t_first = jnp.clip(own - 5 * BLOCK, -BLOCK, total + BLOCK - t_count)
    first, count = block_range(3)
    forward(t_first, t_count, first * BLOCK, count * BLOCK)
    network((h_s, a_s, sino_s), DUAL_SHIFTS, shift_dual, w1d, w2d, first, count)
    update(h_s, DUAL_SHIFTS, shift_dual, first, count)
    first, count = block_range(1)
    adjoint(first * BLOCK, count * BLOCK)
    network((f_s, b_s), PRIMAL_SHIFTS, shift_primal, w1p, w2p, first, count)
    for i in range(row_count // BLOCK):
        slot = own_block - first + i + 1
        base = pl.multiple_of(PAD + own + i * BLOCK, BLOCK)
        for j, value in enumerate(collapse(PRIMAL_SHIFTS, shift_primal, slot)):
            out[i * BLOCK:(i + 1) * BLOCK, j * LANES:(j + 1) * LANES] = f_s[j, pl.ds(base, BLOCK), :] + value


def gather(block, count):
    me = lax.axis_index("gz")
    window = min(count, 2 * HALO_BLOCKS + 1)
    if count & (count - 1) == 0 and count <= window:
        def swap(x, bits):
            return lax.ppermute(x, "gz", [(i, i ^ bits) for i in range(count)])

        held = {0: block}
        for bits in range(2, count, 4):
            held[bits] = swap(block, bits)
        for bits in range(4, count, 4):
            held[bits] = swap(block, bits)
        if count > 1:
            for bits in list(held):
                held[bits ^ 1] = swap(held[bits], 1)
        return [held[b] for b in sorted(held)], [me ^ b for b in sorted(held)], me
    first = jnp.clip(me - HALO_BLOCKS, 0, count - window)
    whole = lax.all_gather(block, "gz", axis=0)
    return [whole[first + j] for j in range(window)], list(range(window)), me - first


def per_device(
    start_volume, sinogram, offsets, projector, dual_in, dual_out, primal_in, primal_out
):
    row_count, cells = start_volume.shape[1:]
    tiles = cells // LANES
    segment = lax.axis_index("segment")
    own_start = start_volume[segment]
    block = jnp.stack([own_start, sinogram[segment]]).astype(jnp.bfloat16)
    pieces, places, own = gather(block, lax.axis_size("gz"))
    window = len(pieces)
    total = window * row_count
    info = jnp.concatenate([
        jnp.stack([jnp.int32(own)] + [jnp.int32(p) for p in places]) * row_count,
        offsets[segment],
    ])
    dual_hidden, primal_hidden = dual_in.shape[0], primal_in.shape[0]
    tables = [
        first_structure(3, 3, 128), second_structure(3, 16), place_structure(dual_hidden),
        first_structure(9, 2, 256), second_structure(9, 32), place_structure(primal_hidden),
    ]
    tables = [jnp.asarray(t, jnp.bfloat16) for t in tables]
    blocks = total // BLOCK
    padded = total + 2 * PAD
    field = pltpu.VMEM((tiles, padded, LANES), jnp.float32)
    whole = pl.BlockSpec(memory_space=pltpu.VMEM)
    operands = [own_start, *pieces, projector.reshape(-1, cells), dual_in, dual_out, primal_in,
                primal_out, *tables]
    result = pl.pallas_call(
        functools.partial(kernel, (window, tiles)),
        out_shape=jax.ShapeDtypeStruct((row_count, cells), jnp.float32),
        in_specs=[pl.BlockSpec(memory_space=pltpu.SMEM)] + [whole] * len(operands),
        out_specs=whole,
        scratch_shapes=[field] * 6 + [
            pltpu.VMEM((256, cells), jnp.bfloat16),
            pltpu.VMEM((min(blocks, 16) + 2, 144, cells), jnp.float32),
            pltpu.VMEM((total + 2 * BLOCK, 3 * cells), jnp.bfloat16),
            pltpu.VMEM((BLOCK * dual_hidden, 128), jnp.bfloat16),
            pltpu.VMEM((48, BLOCK * dual_hidden), jnp.bfloat16),
            pltpu.VMEM((BLOCK * primal_hidden, 256), jnp.bfloat16),
            pltpu.VMEM((144, BLOCK * primal_hidden), jnp.bfloat16),
            pltpu.VMEM((256, BLOCK * primal_hidden), jnp.float32),
        ],
        compiler_params=pltpu.CompilerParams(vmem_limit_bytes=48 * 1024 * 1024),
    )(info, *operands)
    return result[None]


def solution(mesh):
    in_specs = (P(None, "gz", None), P(None, "gz", None), P(), P(), P(), P(), P(), P())
    out_specs = P("segment", "gz", None)
    return jax.shard_map(
        per_device, mesh=mesh, in_specs=in_specs, out_specs=out_specs, check_vma=False
    )
```

```python
import functools

import jax
import jax.numpy as jnp
import numpy as np
from jax import lax
from jax.experimental import pallas as pl
from jax.experimental.pallas import tpu as pltpu
from jax.sharding import PartitionSpec as P

IMG = 32
LANES = 128
BLOCK = 8
PAD = 16
HALO_BLOCKS = 5

DUAL_SHIFTS = (-1, 0, 1)
PRIMAL_SHIFTS = tuple((dy, dx) for dy in (-1, 0, 1) for dx in (-1, 0, 1))


def dot(a, b):
    return jnp.dot(a, b, preferred_element_type=jnp.float32)


def lanes():
    return lax.broadcasted_iota(jnp.int32, (BLOCK, LANES), 1)


def rows_of():
    return lax.broadcasted_iota(jnp.int32, (BLOCK, LANES), 0)


def shift_dual(tiles, step):
    if step == 0:
        return tiles
    lane = lanes()
    keep = (lane + step >= 0) & (lane + step < LANES)
    return [jnp.where(keep, pltpu.roll(t, (-step) % LANES, 1), 0.0) for t in tiles]


def shift_primal(tiles, step):
    dy, dx = step
    offset = dy * IMG + dx
    if offset == 0:
        return tiles
    lane = lanes()
    column = lane % IMG
    inside = (column + dx >= 0) & (column + dx < IMG)
    near = inside & (lane + offset >= 0) & (lane + offset < LANES)
    far = inside & ((lane + offset < 0) | (lane + offset >= LANES))
    rolled = [pltpu.roll(t, (-offset) % LANES, 1) for t in tiles]
    side = 1 if offset > 0 else -1
    out = []
    for j in range(len(tiles)):
        value = jnp.where(near, rolled[j], 0.0)
        if 0 <= j + side < len(tiles):
            value = jnp.where(far, rolled[j + side], value)
        out.append(value)
    return out


def iota(shape, dim):
    return lax.broadcasted_iota(jnp.int32, shape, dim)


def first_weights(w_in, taps, shift_count, channels, out):
    width = out.shape[1]
    hidden = w_in.shape[1]
    arrays = shift_count * channels
    main = arrays * BLOCK
    column = iota((taps, width), 1)
    row = iota((taps, width), 0)
    place = column - main
    outer = lax.bitwise_and(place, BLOCK - 1)
    outer_tap = (place // BLOCK) * channels + outer // 2
    used = (place >= 0) & (place < shift_count * BLOCK) & (outer < 2 * channels)
    low = used & (outer % 2 == 0)
    high = used & (outer % 2 == 1)
    for z in range(BLOCK):
        tap = (column % BLOCK - z + 1) * arrays + column // BLOCK
        hit = (place < 0) & (row == tap)
        if z == 0:
            hit = hit | (low & (row == outer_tap))
        if z == BLOCK - 1:
            hit = hit | (high & (row == outer_tap + 2 * arrays))
        table = jnp.where(hit, 1.0, 0.0).astype(jnp.bfloat16)
        out[z * hidden:(z + 1) * hidden, :] = lax.dot_general(
            w_in, table, (((0,), (0,)), ((), ())), preferred_element_type=jnp.float32
        ).astype(jnp.bfloat16)


def second_weights(w_out, hidden, shift_count, out):
    taps = w_out.shape[0]
    height, wide = out.shape
    spread = jnp.where(iota((hidden, wide), 1) % hidden == iota((hidden, wide), 0), 1.0, 0.0)
    across = dot(w_out, spread.astype(jnp.bfloat16)).astype(jnp.bfloat16)
    place = iota((height, taps), 0)
    tap = iota((height, taps), 1)
    shift = place // (2 * BLOCK)
    inner = (place // BLOCK) % 2 == 0
    row = place % BLOCK
    lane = iota((height, wide), 1) // hidden
    total = jnp.zeros((height, wide), jnp.float32)
    for z in range(BLOCK):
        hit = inner & (tap == (z + 1 - row) * shift_count + shift)
        if z == 0:
            hit = hit | (~inner & (row == BLOCK - 1) & (tap == 2 * shift_count + shift))
        if z == BLOCK - 1:
            hit = hit | (~inner & (row == 0) & (tap == shift))
        part = dot(jnp.where(hit, 1.0, 0.0).astype(jnp.bfloat16), across)
        total = jnp.where(lane == z, part, total)
    out[...] = total.astype(jnp.bfloat16)


def prepare(sizes, weights, w1d, w2d, w1p, w2p):
    (d_taps, d_hidden), (p_taps, p_hidden) = sizes
    at = 0
    parts = []
    for rows, columns in ((d_taps, d_hidden), (d_taps // 3, d_hidden), (p_taps, p_hidden),
                          (p_taps // 2, p_hidden)):
        parts.append(weights[at:at + rows, 0:columns])
        at += -(-rows // 16) * 16
    first_weights(parts[0], d_taps, 3, 3, w1d)
    second_weights(parts[1], d_hidden, 3, w2d)
    first_weights(parts[2], p_taps, 9, 2, w1p)
    second_weights(parts[3], p_hidden, 9, w2p)


def kernel(sizes, info, own_start, *refs):
    window, tiles = sizes
    pieces = refs[:window]
    (projector, w1d, w2d, w1p, w2p, out, f_s, sino_s, t_s, a_s, h_s, b_s, x_0, x_1, hidden_0, hidden_1,
     y_s, lhs_s) = refs[window:]
    x_refs, hidden_refs = (x_0, x_1), (hidden_0, hidden_1)
    row_count = own_start.shape[0]
    total = window * row_count
    blocks = total // BLOCK
    cells = tiles * LANES
    own = info[0]
    own_block = own // BLOCK

    def offset_of(view):
        return info[1 + window + view]

    zero_rows = jnp.zeros((tiles, PAD, LANES), jnp.float32)
    for field in (f_s, sino_s, t_s, a_s):
        field[:, 0:PAD, :] = zero_rows
        field[:, PAD + total:PAD + total + PAD, :] = zero_rows
    h_s[...] = jnp.zeros(h_s.shape, jnp.float32)
    b_s[...] = jnp.zeros(b_s.shape, jnp.float32)
    for x in x_refs:
        x[...] = jnp.zeros(x.shape, jnp.bfloat16)
    for i, piece in enumerate(pieces):
        at = pl.multiple_of(info[1 + i] + PAD, BLOCK)
        for j in range(tiles):
            cut = slice(j * LANES, (j + 1) * LANES)
            f_s[j, pl.ds(at, row_count), :] = piece[0, :, cut].astype(jnp.float32)
            sino_s[j, pl.ds(at, row_count), :] = piece[1, :, cut].astype(jnp.float32)
    for j in range(tiles):
        f_s[j, pl.ds(pl.multiple_of(own + PAD, BLOCK), row_count), :] = own_start[:, j * LANES:(j + 1) * LANES]

    def forward(first_row, count, z_first, z_count):
        for k in range(3):
            for j in range(tiles):
                lhs_s[0:count, k * cells + j * LANES:k * cells + (j + 1) * LANES] = f_s[
                    j, pl.ds(PAD + first_row + (k - 1), count), :].astype(jnp.bfloat16)
        for n in range(cells // 256):
            value = dot(lhs_s[0:count, :], projector[:, n * 256:(n + 1) * 256])
            for part in range(2):
                t_s[2 * n + part, pl.ds(pl.multiple_of(PAD + first_row, BLOCK), count), :] = value[
                    :, part * LANES:(part + 1) * LANES]
        for w in range(tiles):
            a_s[w, pl.ds(pl.multiple_of(PAD + z_first, BLOCK), z_count), :] = t_s[
                w, pl.ds(PAD + z_first + offset_of(w), z_count), :]

    def adjoint(z_first, count):
        for k in range(3):
            for w in range(tiles):
                lhs_s[0:count, k * cells + w * LANES:k * cells + (w + 1) * LANES] = h_s[
                    w, pl.ds(PAD + z_first - offset_of(w) - (k - 1), count), :].astype(jnp.bfloat16)
        for n in range(cells // 256):
            value = jnp.zeros((count, 256), jnp.float32)
            for k in range(3):
                value = value + lax.dot_general(
                    lhs_s[0:count, k * cells:(k + 1) * cells],
                    projector[k * cells + n * 256:k * cells + (n + 1) * 256, :],
                    (((1,), (1,)), ((), ())), preferred_element_type=jnp.float32)
            for part in range(2):
                b_s[2 * n + part, pl.ds(pl.multiple_of(PAD + z_first, BLOCK), count), :] = value[
                    :, part * LANES:(part + 1) * LANES]

    def network(fields, shifts, shift_tiles, w1, w2, block_first, block_count):
        count = len(shifts)
        hidden_rows, depth = w1.shape
        out_rows = 2 * BLOCK * count
        edge = jnp.zeros((out_rows, cells), jnp.float32)
        y_s[0, 0:out_rows, :] = edge
        y_s[block_count + 1, 0:out_rows, :] = edge

        def build_taps(x, base):
            row = rows_of()
            mains = [[field[j, pl.ds(base, BLOCK), :] for j in range(tiles)] for field in fields]
            edges = []
            for j in range(tiles):
                value = jnp.zeros((BLOCK, LANES), jnp.float32)
                for c, field in enumerate(fields):
                    value = jnp.where(row == 2 * c, field[j, pl.ds(base - 1 - 2 * c, BLOCK), :], value)
                    value = jnp.where(row == 2 * c + 1, field[j, pl.ds(base + BLOCK - 1 - 2 * c, BLOCK), :], value)
                edges.append(value)
            arrays = [shift_tiles(main, s) for s in shifts for main in mains]
            arrays += [shift_tiles(edges, s) for s in shifts]
            if len(arrays) % 2:
                arrays.append([jnp.zeros((BLOCK, LANES), jnp.float32)] * tiles)
            for pair in range(len(arrays) // 2):
                for j in range(tiles):
                    x[pair * 16:(pair + 1) * 16, j * LANES:(j + 1) * LANES] = jnp.concatenate(
                        [arrays[2 * pair][j], arrays[2 * pair + 1][j]], axis=0).astype(jnp.bfloat16)

        group = len(x_refs)

        @pl.loop(0, block_count // group)
        def _(i):
            for u in range(group):
                build_taps(x_refs[u], pl.multiple_of(PAD + (block_first + i * group + u) * BLOCK, BLOCK))
            for u in range(group):
                hidden = dot(w1[...], x_refs[u][0:depth, :]).astype(jnp.bfloat16)
                hidden_refs[u][0:hidden_rows, :] = jnp.maximum(hidden, jnp.zeros_like(hidden))
            for u in range(group):
                y_s[i * group + u + 1, 0:out_rows, :] = dot(w2[...], hidden_refs[u][0:hidden_rows, :])

    def collapse(shifts, shift_tiles, slot):
        row = rows_of()
        total_value = None
        for s, step in enumerate(shifts):
            at = s * 2 * BLOCK
            merged = []
            for j in range(tiles):
                cut = slice(j * LANES, (j + 1) * LANES)
                outer = jnp.where(row == 0, y_s[slot - 1, at + BLOCK:at + 2 * BLOCK, cut], 0.0)
                outer = jnp.where(row == BLOCK - 1, y_s[slot + 1, at + BLOCK:at + 2 * BLOCK, cut], outer)
                merged.append(y_s[slot, at:at + BLOCK, cut] + outer)
            moved = shift_tiles(merged, step)
            total_value = moved if total_value is None else [a + b for a, b in zip(total_value, moved)]
        return total_value

    def update(field, shifts, shift_tiles, block_first, block_count):
        @pl.loop(0, block_count)
        def _(i):
            base = pl.multiple_of(PAD + (block_first + i) * BLOCK, BLOCK)
            for j, value in enumerate(collapse(shifts, shift_tiles, i + 1)):
                field[j, pl.ds(base, BLOCK), :] += value

    def block_range(reach, own_count=row_count // BLOCK):
        count = min(blocks, own_count + 2 * reach)
        return jnp.clip(own_block - reach, 0, blocks - count), count

    first, count = block_range(7)
    forward(jnp.int32(-BLOCK), total + 2 * BLOCK, 0, total)
    network((h_s, a_s, sino_s), DUAL_SHIFTS, shift_dual, w1d, w2d, first, count)
    update(h_s, DUAL_SHIFTS, shift_dual, first, count)
    first, count = block_range(5)
    adjoint(first * BLOCK, count * BLOCK)
    network((f_s, b_s), PRIMAL_SHIFTS, shift_primal, w1p, w2p, first, count)
    update(f_s, PRIMAL_SHIFTS, shift_primal, first, count)

    t_count = min(total + 2 * BLOCK, row_count + 10 * BLOCK)
    t_first = jnp.clip(own - 5 * BLOCK, -BLOCK, total + BLOCK - t_count)
    first, count = block_range(3)
    forward(t_first, t_count, first * BLOCK, count * BLOCK)
    network((h_s, a_s, sino_s), DUAL_SHIFTS, shift_dual, w1d, w2d, first, count)
    update(h_s, DUAL_SHIFTS, shift_dual, first, count)
    first, count = block_range(1)
    adjoint(first * BLOCK, count * BLOCK)
    network((f_s, b_s), PRIMAL_SHIFTS, shift_primal, w1p, w2p, first, count)
    for i in range(row_count // BLOCK):
        slot = own_block - first + i + 1
        base = pl.multiple_of(PAD + own + i * BLOCK, BLOCK)
        for j, value in enumerate(collapse(PRIMAL_SHIFTS, shift_primal, slot)):
            out[i * BLOCK:(i + 1) * BLOCK, j * LANES:(j + 1) * LANES] = f_s[j, pl.ds(base, BLOCK), :] + value

def gather(block, count):
    me = lax.axis_index("gz")
    window = min(count, 2 * HALO_BLOCKS + 1)
    if count & (count - 1) == 0 and count <= window:
        def swap(x, bits):
            return lax.ppermute(x, "gz", [(i, i ^ bits) for i in range(count)])

        held = {0: block}
        for bits in range(2, count, 4):
            held[bits] = swap(block, bits)
        for bits in range(4, count, 4):
            held[bits] = swap(block, bits)
        if count > 1:
            for bits in list(held):
                held[bits ^ 1] = swap(held[bits], 1)
        return [held[b] for b in sorted(held)], [me ^ b for b in sorted(held)], me
    first = jnp.clip(me - HALO_BLOCKS, 0, count - window)
    whole = lax.all_gather(block, "gz", axis=0)
    return [whole[first + j] for j in range(window)], list(range(window)), me - first


def per_device(
    start_volume, sinogram, offsets, projector, dual_in, dual_out, primal_in, primal_out
):
    row_count, cells = start_volume.shape[1:]
    tiles = cells // LANES
    segment = lax.axis_index("segment")
    own_start = start_volume[segment]
    block = jnp.stack([own_start, sinogram[segment]]).astype(jnp.bfloat16)
    pieces, places, own = gather(block, lax.axis_size("gz"))
    window = len(pieces)
    total = window * row_count
    info = jnp.concatenate([
        jnp.stack([jnp.int32(own)] + [jnp.int32(p) for p in places]) * row_count,
        offsets[segment],
    ])
    dual_hidden, primal_hidden = dual_in.shape[0], primal_in.shape[0]
    parts = [dual_in.T, dual_out, primal_in.T, primal_out]
    packed = jnp.concatenate([
        jnp.pad(p, ((0, -p.shape[0] % 16), (0, primal_hidden - p.shape[1]))) for p in parts])
    blocks = total // BLOCK
    padded = total + 2 * PAD
    field = pltpu.VMEM((tiles, padded, LANES), jnp.float32)
    whole = pl.BlockSpec(memory_space=pltpu.VMEM)
    flat = projector.reshape(-1, cells)
    weights = pl.pallas_call(
        functools.partial(prepare, (dual_in.shape[::-1], primal_in.shape[::-1])),
        out_shape=[
            jax.ShapeDtypeStruct(shape, jnp.bfloat16) for shape in (
                (BLOCK * dual_hidden, 128), (48, BLOCK * dual_hidden),
                (BLOCK * primal_hidden, 256), (144, BLOCK * primal_hidden))
        ],
        in_specs=[whole],
        out_specs=[whole] * 4,
        cost_estimate=pl.CostEstimate(flops=2_000_000_000, bytes_accessed=8_000_000, transcendentals=0),
        compiler_params=pltpu.CompilerParams(vmem_limit_bytes=16 * 1024 * 1024),
        name="prepare",
    )(packed)
    operands = [own_start, *pieces, flat, *weights]
    result = pl.pallas_call(
        functools.partial(kernel, (window, tiles)),
        out_shape=jax.ShapeDtypeStruct((row_count, cells), jnp.float32),
        in_specs=[pl.BlockSpec(memory_space=pltpu.SMEM)] + [whole] * len(operands),
        out_specs=whole,
        scratch_shapes=[field] * 6 + [
            pltpu.VMEM((256, cells), jnp.bfloat16),
            pltpu.VMEM((256, cells), jnp.bfloat16),
            pltpu.VMEM((BLOCK * primal_hidden, cells), jnp.bfloat16),
            pltpu.VMEM((BLOCK * primal_hidden, cells), jnp.bfloat16),
            pltpu.VMEM((min(blocks, 16) + 2, 144, cells), jnp.float32),
            pltpu.VMEM((total + 2 * BLOCK, 3 * cells), jnp.bfloat16),
        ],
        compiler_params=pltpu.CompilerParams(vmem_limit_bytes=32 * 1024 * 1024),
        name="iterate",
    )(info, *operands)
    return result[None]


def solution(mesh):
    in_specs = (P(None, "gz", None), P(None, "gz", None), P(), P(), P(), P(), P(), P())
    out_specs = P("segment", "gz", None)
    return jax.shard_map(
        per_device, mesh=mesh, in_specs=in_specs, out_specs=out_specs, check_vma=False
    )
```

```python
import functools

import jax
import jax.numpy as jnp
import numpy as np
from jax import lax
from jax.experimental import pallas as pl
from jax.experimental.pallas import tpu as pltpu
from jax.sharding import PartitionSpec as P

IMG = 32
LANES = 128
BLOCK = 8
PAD = 16
HALO_BLOCKS = 5
LAG = 4


def dot(a, b):
    return jnp.dot(a, b, preferred_element_type=jnp.float32)


def lanes():
    return lax.broadcasted_iota(jnp.int32, (BLOCK, LANES), 1)


def rows_of():
    return lax.broadcasted_iota(jnp.int32, (BLOCK, LANES), 0)


def masks_of():
    lane = lanes()
    row = rows_of()
    column = lane % IMG
    return {
        "view": {-1: lane > 0, 1: lane < LANES - 1},
        "across": {-1: column > 0, 1: column < IMG - 1},
        "down": {-1: lane >= IMG, 1: lane < LANES - IMG},
        "rows": [row == r for r in range(BLOCK)],
    }


def shift_lanes(tiles, step, mask):
    return [jnp.where(mask, pltpu.roll(t, (-step) % LANES, 1), 0.0) for t in tiles]


def shift_down(tiles, dy, mask):
    rolled = [pltpu.roll(t, (-dy * IMG) % LANES, 1) for t in tiles]
    zero = jnp.zeros_like(tiles[0])
    beyond = rolled[1:] + [zero] if dy > 0 else [zero] + rolled[:-1]
    return [jnp.where(mask, near, far) for near, far in zip(rolled, beyond)]


def dual_shifted(tiles, masks):
    return [shift_lanes(tiles, -1, masks["view"][-1]), tiles, shift_lanes(tiles, 1, masks["view"][1])]


def dual_sum(values, masks):
    return add(add(shift_lanes(values(0), -1, masks["view"][-1]), values(1)),
               shift_lanes(values(2), 1, masks["view"][1]))


def primal_shifted(tiles, masks):
    across = [shift_lanes(tiles, -1, masks["across"][-1]), tiles, shift_lanes(tiles, 1, masks["across"][1])]
    return ([shift_down(t, -1, masks["down"][-1]) for t in across] + across
            + [shift_down(t, 1, masks["down"][1]) for t in across])


def primal_sum(values, masks):
    total = None
    for dy in (-1, 0, 1):
        at = (dy + 1) * 3
        part = add(add(shift_lanes(values(at), -1, masks["across"][-1]), values(at + 1)),
                   shift_lanes(values(at + 2), 1, masks["across"][1]))
        if dy:
            part = shift_down(part, dy, masks["down"][dy])
        total = part if total is None else add(total, part)
    return total


def add(a, b):
    return [x + y for x, y in zip(a, b)]


DUAL = (3, dual_shifted, dual_sum)
PRIMAL = (9, primal_shifted, primal_sum)


def iota(shape, dim):
    return lax.broadcasted_iota(jnp.int32, shape, dim)


def first_weights(w_in, taps, shift_count, channels, out):
    width = out.shape[1]
    hidden = w_in.shape[1]
    arrays = shift_count * channels
    main = arrays * BLOCK
    column = iota((taps, width), 1)
    row = iota((taps, width), 0)
    place = column - main
    outer = lax.bitwise_and(place, BLOCK - 1)
    outer_tap = (place // BLOCK) * channels + outer // 2
    used = (place >= 0) & (place < shift_count * BLOCK) & (outer < 2 * channels)
    low = used & (outer % 2 == 0)
    high = used & (outer % 2 == 1)
    for z in range(BLOCK):
        tap = (column % BLOCK - z + 1) * arrays + column // BLOCK
        hit = (place < 0) & (row == tap)
        if z == 0:
            hit = hit | (low & (row == outer_tap))
        if z == BLOCK - 1:
            hit = hit | (high & (row == outer_tap + 2 * arrays))
        table = jnp.where(hit, 1.0, 0.0).astype(jnp.bfloat16)
        out[z * hidden:(z + 1) * hidden, :] = lax.dot_general(
            w_in, table, (((0,), (0,)), ((), ())), preferred_element_type=jnp.float32
        ).astype(jnp.bfloat16)


def second_weights(w_out, hidden, shift_count, out):
    taps = w_out.shape[0]
    height, wide = out.shape
    spread = jnp.where(iota((hidden, wide), 1) % hidden == iota((hidden, wide), 0), 1.0, 0.0)
    across = dot(w_out, spread.astype(jnp.bfloat16)).astype(jnp.bfloat16)
    place = iota((height, taps), 0)
    tap = iota((height, taps), 1)
    shift = place // (2 * BLOCK)
    inner = (place // BLOCK) % 2 == 0
    row = place % BLOCK
    lane = iota((height, wide), 1) // hidden
    total = jnp.zeros((height, wide), jnp.float32)
    for z in range(BLOCK):
        hit = inner & (tap == (z + 1 - row) * shift_count + shift)
        if z == 0:
            hit = hit | (~inner & (row == BLOCK - 1) & (tap == 2 * shift_count + shift))
        if z == BLOCK - 1:
            hit = hit | (~inner & (row == 0) & (tap == shift))
        part = dot(jnp.where(hit, 1.0, 0.0).astype(jnp.bfloat16), across)
        total = jnp.where(lane == z, part, total)
    out[...] = total.astype(jnp.bfloat16)


def prepare(sizes, weights, w1d, w2d, w1p, w2p):
    (d_taps, d_hidden), (p_taps, p_hidden) = sizes
    at = 0
    parts = []
    for rows, columns in ((d_taps, d_hidden), (d_taps // 3, d_hidden), (p_taps, p_hidden),
                          (p_taps // 2, p_hidden)):
        parts.append(weights[at:at + rows, 0:columns])
        at += -(-rows // 16) * 16
    first_weights(parts[0], d_taps, 3, 3, w1d)
    second_weights(parts[1], d_hidden, 3, w2d)
    first_weights(parts[2], p_taps, 9, 2, w1p)
    second_weights(parts[3], p_hidden, 9, w2p)


def kernel(sizes, info, own_start, *refs):
    window, tiles = sizes
    pieces = refs[:window]
    (projector, w1d, w2d, w1p, w2p, out, f_s, sino_s, t_s, a_s, h_s, b_s,
     x_0, x_1, x_2, x_3, hidden_0, hidden_1, hidden_2, hidden_3, y_s, lhs_s,
     across_s) = refs[window:]
    x_refs, hidden_refs = ((x_0, x_1), (x_2, x_3)), ((hidden_0, hidden_1), (hidden_2, hidden_3))
    row_count = own_start.shape[0]
    total = window * row_count
    blocks = total // BLOCK
    cells = tiles * LANES
    own = info[0]
    own_block = own // BLOCK

    masks = masks_of()

    def offset_of(view):
        return info[1 + window + view]

    zero_rows = jnp.zeros((tiles, PAD, LANES), jnp.float32)
    for field in (f_s, sino_s, t_s, a_s):
        field[:, 0:PAD, :] = zero_rows
        field[:, PAD + total:PAD + total + PAD, :] = zero_rows
    h_s[...] = jnp.zeros(h_s.shape, jnp.float32)
    b_s[...] = jnp.zeros(b_s.shape, jnp.float32)
    for i, piece in enumerate(pieces):
        at = pl.multiple_of(info[1 + i] + PAD, BLOCK)
        for j in range(tiles):
            cut = slice(j * LANES, (j + 1) * LANES)
            f_s[j, pl.ds(at, row_count), :] = piece[0, :, cut].astype(jnp.float32)
            sino_s[j, pl.ds(at, row_count), :] = piece[1, :, cut].astype(jnp.float32)
    for j in range(tiles):
        f_s[j, pl.ds(pl.multiple_of(own + PAD, BLOCK), row_count), :] = own_start[:, j * LANES:(j + 1) * LANES]

    def forward(first_row, count, z_first, z_count):
        for k in range(3):
            for j in range(tiles):
                lhs_s[0:count, k * cells + j * LANES:k * cells + (j + 1) * LANES] = f_s[
                    j, pl.ds(PAD + first_row + (k - 1), count), :].astype(jnp.bfloat16)
        for n in range(cells // 256):
            value = dot(lhs_s[0:count, :], projector[:, n * 256:(n + 1) * 256])
            for part in range(2):
                t_s[2 * n + part, pl.ds(pl.multiple_of(PAD + first_row, BLOCK), count), :] = value[
                    :, part * LANES:(part + 1) * LANES]
        for w in range(tiles):
            a_s[w, pl.ds(pl.multiple_of(PAD + z_first, BLOCK), z_count), :] = t_s[
                w, pl.ds(PAD + z_first + offset_of(w), z_count), :]

    def transpose_part(n):
        columns = pl.ds(pl.multiple_of(n * 256, 256), 256)
        for k in range(3):
            rows = pl.ds(pl.multiple_of(k * cells + n * 256, 256), 256)
            for m in range(cells // 256):
                at = k * cells + m * 256
                across_s[rows, m * 256:(m + 1) * 256] = projector[at:at + 256, columns].T

    def adjoint(z_first, count):
        for k in range(3):
            for w in range(tiles):
                lhs_s[0:count, k * cells + w * LANES:k * cells + (w + 1) * LANES] = h_s[
                    w, pl.ds(PAD + z_first - offset_of(w) - (k - 1), count), :].astype(jnp.bfloat16)
        for n in range(cells // 256):
            value = dot(lhs_s[0:count, :], across_s[:, n * 256:(n + 1) * 256])
            for part in range(2):
                b_s[2 * n + part, pl.ds(pl.multiple_of(PAD + z_first, BLOCK), count), :] = value[
                    :, part * LANES:(part + 1) * LANES]

    def network(fields, plane, w1, w2, block_first, block_count, target=None, beside=None):
        count, shifted, _ = plane
        hidden_rows, depth = w1.shape
        out_rows = 2 * BLOCK * count
        group = len(x_refs[0])
        groups = block_count // group
        edge = jnp.zeros((out_rows, cells), jnp.float32)
        for slot in (LAG - 1, block_count + LAG):
            y_s[slot, 0:out_rows, :] = edge

        def build_taps(x, block):
            base = pl.multiple_of(PAD + (block_first + block) * BLOCK, BLOCK)
            mains = [[field[j, pl.ds(base, BLOCK), :] for j in range(tiles)] for field in fields]
            edges = []
            for j in range(tiles):
                value = jnp.zeros((BLOCK, LANES), jnp.float32)
                for c, field in enumerate(fields):
                    value = jnp.where(masks["rows"][2 * c], field[j, pl.ds(base - 1 - 2 * c, BLOCK), :], value)
                    value = jnp.where(masks["rows"][2 * c + 1], field[j, pl.ds(base + BLOCK - 1 - 2 * c, BLOCK), :], value)
                edges.append(value)
            moved = [shifted(main, masks) for main in mains]
            arrays = [each[s] for s in range(count) for each in moved] + shifted(edges, masks)
            if len(arrays) % 2:
                arrays.append([jnp.zeros((BLOCK, LANES), jnp.float32)] * tiles)
            for pair in range(len(arrays) // 2):
                for j in range(tiles):
                    x[pair * 16:(pair + 1) * 16, j * LANES:(j + 1) * LANES] = jnp.concatenate(
                        [arrays[2 * pair][j], arrays[2 * pair + 1][j]], axis=0).astype(jnp.bfloat16)

        def add_block(block, guarded):
            value = collapse(plane, block + LAG)
            at = jnp.maximum(block, 0) if guarded else block
            base = pl.multiple_of(PAD + (block_first + at) * BLOCK, BLOCK)
            for j in range(tiles):
                part = jnp.where(block >= 0, value[j], 0.0) if guarded else value[j]
                target[j, pl.ds(base, BLOCK), :] += part

        for u in range(group):
            build_taps(x_refs[0][u], u)

        @pl.loop(0, groups // 2)
        def _(i):
            for phase in range(2):
                now = (2 * i + phase) * group
                after = jnp.minimum(now + group, block_count - group)
                for u in range(group):
                    hidden = dot(w1[...], x_refs[phase][u][0:depth, :]).astype(jnp.bfloat16)
                    hidden_refs[phase][u][0:hidden_rows, :] = jnp.maximum(hidden, jnp.zeros_like(hidden))
                    build_taps(x_refs[1 - phase][u], after + u)
                if target is not None:
                    for u in range(group):
                        add_block(now + u - group - 1, True)
                if beside is not None and phase == 0:
                    beside(i)
                for u in range(group):
                    y_s[now + u + LAG, 0:out_rows, :] = dot(w2[...], hidden_refs[phase][u][0:hidden_rows, :])

        if target is not None:
            for block in range(block_count - group - 1, block_count):
                add_block(block, False)

    def collapse(plane, slot):
        def merged(s):
            at = s * 2 * BLOCK
            out = []
            for j in range(tiles):
                cut = slice(j * LANES, (j + 1) * LANES)
                outer = jnp.where(masks["rows"][0], y_s[slot - 1, at + BLOCK:at + 2 * BLOCK, cut], 0.0)
                outer = jnp.where(masks["rows"][BLOCK - 1], y_s[slot + 1, at + BLOCK:at + 2 * BLOCK, cut], outer)
                out.append(y_s[slot, at:at + BLOCK, cut] + outer)
            return out

        return plane[2](merged, masks)

    def block_range(reach, own_count=row_count // BLOCK):
        count = min(blocks, own_count + 2 * reach)
        return jnp.clip(own_block - reach, 0, blocks - count), count

    first, count = block_range(7)
    forward(jnp.int32(-BLOCK), total + 2 * BLOCK, 0, total)
    if count // 4 == cells // 256:
        network((h_s, a_s, sino_s), DUAL, w1d, w2d, first, count, h_s, transpose_part)
    else:
        network((h_s, a_s, sino_s), DUAL, w1d, w2d, first, count, h_s)
        for n in range(cells // 256):
            transpose_part(n)
    first, count = block_range(5)
    adjoint(first * BLOCK, count * BLOCK)
    network((f_s, b_s), PRIMAL, w1p, w2p, first, count, f_s)

    t_count = min(total + 2 * BLOCK, row_count + 10 * BLOCK)
    t_first = jnp.clip(own - 5 * BLOCK, -BLOCK, total + BLOCK - t_count)
    first, count = block_range(3)
    forward(t_first, t_count, first * BLOCK, count * BLOCK)
    network((h_s, a_s, sino_s), DUAL, w1d, w2d, first, count, h_s)
    first, count = block_range(1)
    adjoint(first * BLOCK, count * BLOCK)
    network((f_s, b_s), PRIMAL, w1p, w2p, first, count)
    for i in range(row_count // BLOCK):
        slot = own_block - first + i + LAG
        base = pl.multiple_of(PAD + own + i * BLOCK, BLOCK)
        for j, value in enumerate(collapse(PRIMAL, slot)):
            out[i * BLOCK:(i + 1) * BLOCK, j * LANES:(j + 1) * LANES] = f_s[j, pl.ds(base, BLOCK), :] + value

def gather(block, count):
    me = lax.axis_index("gz")
    window = min(count, 2 * HALO_BLOCKS + 1)
    if count & (count - 1) == 0 and count <= window:
        def swap(x, bits):
            return lax.ppermute(x, "gz", [(i, i ^ bits) for i in range(count)])

        held = {0: block}
        for bits in range(2, count, 4):
            held[bits] = swap(block, bits)
        for bits in range(4, count, 4):
            held[bits] = swap(block, bits)
        if count > 1:
            for bits in list(held):
                held[bits ^ 1] = swap(held[bits], 1)
        return [held[b] for b in sorted(held)], [me ^ b for b in sorted(held)], me
    first = jnp.clip(me - HALO_BLOCKS, 0, count - window)
    whole = lax.all_gather(block, "gz", axis=0)
    return [whole[first + j] for j in range(window)], list(range(window)), me - first


def per_device(
    start_volume, sinogram, offsets, projector, dual_in, dual_out, primal_in, primal_out
):
    row_count, cells = start_volume.shape[1:]
    tiles = cells // LANES
    segment = lax.axis_index("segment")
    own_start = start_volume[segment]
    block = jnp.stack([own_start, sinogram[segment]]).astype(jnp.bfloat16)
    pieces, places, own = gather(block, lax.axis_size("gz"))
    window = len(pieces)
    total = window * row_count
    info = jnp.concatenate([
        jnp.stack([jnp.int32(own)] + [jnp.int32(p) for p in places]) * row_count,
        offsets[segment],
    ])
    dual_hidden, primal_hidden = dual_in.shape[0], primal_in.shape[0]
    parts = [dual_in.T, dual_out, primal_in.T, primal_out]
    packed = jnp.concatenate([
        jnp.pad(p, ((0, -p.shape[0] % 16), (0, primal_hidden - p.shape[1]))) for p in parts])
    blocks = total // BLOCK
    padded = total + 2 * PAD
    field = pltpu.VMEM((tiles, padded, LANES), jnp.float32)
    whole = pl.BlockSpec(memory_space=pltpu.VMEM)
    flat = projector.reshape(-1, cells)
    weights = pl.pallas_call(
        functools.partial(prepare, (dual_in.shape[::-1], primal_in.shape[::-1])),
        out_shape=[
            jax.ShapeDtypeStruct(shape, jnp.bfloat16) for shape in (
                (BLOCK * dual_hidden, 96), (48, BLOCK * dual_hidden),
                (BLOCK * primal_hidden, 224), (144, BLOCK * primal_hidden))
        ],
        in_specs=[whole],
        out_specs=[whole] * 4,
        cost_estimate=pl.CostEstimate(flops=2_000_000_000, bytes_accessed=8_000_000, transcendentals=0),
        compiler_params=pltpu.CompilerParams(vmem_limit_bytes=16 * 1024 * 1024),
        name="prepare",
    )(packed)
    operands = [own_start, *pieces, flat, *weights]
    result = pl.pallas_call(
        functools.partial(kernel, (window, tiles)),
        out_shape=jax.ShapeDtypeStruct((row_count, cells), jnp.float32),
        in_specs=[pl.BlockSpec(memory_space=pltpu.SMEM)] + [whole] * len(operands),
        out_specs=whole,
        scratch_shapes=[field] * 6 + [
            *[pltpu.VMEM((224, cells), jnp.bfloat16)] * 4,
            *[pltpu.VMEM((BLOCK * primal_hidden, cells), jnp.bfloat16)] * 4,
            pltpu.VMEM((min(blocks, 16) + LAG + 1, 144, cells), jnp.float32),
            pltpu.VMEM((total + 2 * BLOCK, 3 * cells), jnp.bfloat16),
            pltpu.VMEM((3 * cells, cells), jnp.bfloat16),
        ],
        compiler_params=pltpu.CompilerParams(vmem_limit_bytes=32 * 1024 * 1024),
        name="iterate",
    )(info, *operands)
    return result[None]


def solution(mesh):
    in_specs = (P(None, "gz", None), P(None, "gz", None), P(), P(), P(), P(), P(), P())
    out_specs = P("segment", "gz", None)
    return jax.shard_map(
        per_device, mesh=mesh, in_specs=in_specs, out_specs=out_specs, check_vma=False
    )
```

```python
import functools

import jax
import jax.numpy as jnp
import numpy as np
from jax import lax
from jax.experimental import pallas as pl
from jax.experimental.pallas import tpu as pltpu
from jax.sharding import PartitionSpec as P

IMG = 32
LANES = 128
BLOCK = 8
PAD = 16
HALO_BLOCKS = 5
LAG = 4
STEPS = 2
UNROLLED = 12


def dot(a, b):
    return jnp.dot(a, b, preferred_element_type=jnp.float32)


def lanes():
    return lax.broadcasted_iota(jnp.int32, (BLOCK, LANES), 1)


def rows_of():
    return lax.broadcasted_iota(jnp.int32, (BLOCK, LANES), 0)


def masks_of():
    lane = lanes()
    row = rows_of()
    column = lane % IMG
    return {
        "view": {-1: lane > 0, 1: lane < LANES - 1},
        "across": {-1: column > 0, 1: column < IMG - 1},
        "down": {-1: lane >= IMG, 1: lane < LANES - IMG},
        "rows": [row == r for r in range(BLOCK)],
    }


def shift_lanes(tiles, step, mask):
    return [jnp.where(mask, pltpu.roll(t, (-step) % LANES, 1), 0.0) for t in tiles]


def shift_down(tiles, dy, mask):
    rolled = [pltpu.roll(t, (-dy * IMG) % LANES, 1) for t in tiles]
    zero = jnp.zeros_like(tiles[0])
    beyond = rolled[1:] + [zero] if dy > 0 else [zero] + rolled[:-1]
    return [jnp.where(mask, near, far) for near, far in zip(rolled, beyond)]


def dual_shifted(tiles, masks):
    return [shift_lanes(tiles, -1, masks["view"][-1]), tiles, shift_lanes(tiles, 1, masks["view"][1])]


def dual_sum(values, masks):
    return add(add(shift_lanes(values(0), -1, masks["view"][-1]), values(1)),
               shift_lanes(values(2), 1, masks["view"][1]))


def primal_shifted(tiles, masks):
    across = [shift_lanes(tiles, -1, masks["across"][-1]), tiles, shift_lanes(tiles, 1, masks["across"][1])]
    return ([shift_down(t, -1, masks["down"][-1]) for t in across] + across
            + [shift_down(t, 1, masks["down"][1]) for t in across])


def primal_sum(values, masks):
    total = None
    for dy in (-1, 0, 1):
        at = (dy + 1) * 3
        part = add(add(shift_lanes(values(at), -1, masks["across"][-1]), values(at + 1)),
                   shift_lanes(values(at + 2), 1, masks["across"][1]))
        if dy:
            part = shift_down(part, dy, masks["down"][dy])
        total = part if total is None else add(total, part)
    return total


def add(a, b):
    return [x + y for x, y in zip(a, b)]


DUAL = (3, dual_shifted, dual_sum)
PRIMAL = (9, primal_shifted, primal_sum)


def iota(shape, dim):
    return lax.broadcasted_iota(jnp.int32, shape, dim)


def first_weights(w_in, taps, shift_count, channels, out):
    width = out.shape[1]
    hidden = w_in.shape[1]
    arrays = shift_count * channels
    main = arrays * BLOCK
    column = iota((taps, width), 1)
    row = iota((taps, width), 0)
    place = column - main
    outer = lax.bitwise_and(place, BLOCK - 1)
    outer_tap = (place // BLOCK) * channels + outer // 2
    used = (place >= 0) & (place < shift_count * BLOCK) & (outer < 2 * channels)
    low = used & (outer % 2 == 0)
    high = used & (outer % 2 == 1)
    for z in range(BLOCK):
        tap = (column % BLOCK - z + 1) * arrays + column // BLOCK
        hit = (place < 0) & (row == tap)
        if z == 0:
            hit = hit | (low & (row == outer_tap))
        if z == BLOCK - 1:
            hit = hit | (high & (row == outer_tap + 2 * arrays))
        table = jnp.where(hit, 1.0, 0.0).astype(jnp.bfloat16)
        out[z * hidden:(z + 1) * hidden, :] = lax.dot_general(
            w_in, table, (((0,), (0,)), ((), ())), preferred_element_type=jnp.float32
        ).astype(jnp.bfloat16)


def second_weights(w_out, hidden, shift_count, out):
    taps = w_out.shape[0]
    height, wide = out.shape
    spread = jnp.where(iota((hidden, wide), 1) % hidden == iota((hidden, wide), 0), 1.0, 0.0)
    across = dot(w_out, spread.astype(jnp.bfloat16)).astype(jnp.bfloat16)
    place = iota((height, taps), 0)
    tap = iota((height, taps), 1)
    shift = place // (2 * BLOCK)
    inner = (place // BLOCK) % 2 == 0
    row = place % BLOCK
    lane = iota((height, wide), 1) // hidden
    total = jnp.zeros((height, wide), jnp.float32)
    for z in range(BLOCK):
        hit = inner & (tap == (z + 1 - row) * shift_count + shift)
        if z == 0:
            hit = hit | (~inner & (row == BLOCK - 1) & (tap == 2 * shift_count + shift))
        if z == BLOCK - 1:
            hit = hit | (~inner & (row == 0) & (tap == shift))
        part = dot(jnp.where(hit, 1.0, 0.0).astype(jnp.bfloat16), across)
        total = jnp.where(lane == z, part, total)
    out[...] = total.astype(jnp.bfloat16)


def prepare(sizes, weights, w1d, w2d, w1p, w2p):
    (d_taps, d_hidden), (p_taps, p_hidden) = sizes
    at = 0
    parts = []
    for rows, columns in ((d_taps, d_hidden), (d_taps // 3, d_hidden), (p_taps, p_hidden),
                          (p_taps // 2, p_hidden)):
        parts.append(weights[at:at + rows, 0:columns])
        at += -(-rows // 16) * 16
    first_weights(parts[0], d_taps, 3, 3, w1d)
    second_weights(parts[1], d_hidden, 3, w2d)
    first_weights(parts[2], p_taps, 9, 2, w1p)
    second_weights(parts[3], p_hidden, 9, w2p)


def kernel(sizes, info, own_start, *refs):
    window, tiles = sizes
    pieces = refs[:window]
    (projector, w1d, w2d, w1p, w2p, out, f_s, sino_s, t_s, a_s, h_s, b_s,
     x_0, x_1, x_2, x_3, hidden_0, hidden_1, hidden_2, hidden_3, y_s, lhs_s,
     across_s) = refs[window:]
    x_refs, hidden_refs = ((x_0, x_1), (x_2, x_3)), ((hidden_0, hidden_1), (hidden_2, hidden_3))
    row_count = own_start.shape[0]
    total = window * row_count
    cells = tiles * LANES
    own = info[0]

    masks = masks_of()

    def offset_of(view):
        return info[1 + window + view]

    zero_rows = jnp.zeros((tiles, PAD, LANES), jnp.float32)
    for field in (f_s, sino_s, t_s, a_s):
        field[:, 0:PAD, :] = zero_rows
        field[:, PAD + total:PAD + total + PAD, :] = zero_rows
    h_s[...] = jnp.zeros(h_s.shape, jnp.float32)
    b_s[...] = jnp.zeros(b_s.shape, jnp.float32)
    for i, piece in enumerate(pieces):
        at = pl.multiple_of(info[1 + i] + PAD, BLOCK)
        for j in range(tiles):
            cut = slice(j * LANES, (j + 1) * LANES)
            f_s[j, pl.ds(at, row_count), :] = piece[0, :, cut].astype(jnp.float32)
            sino_s[j, pl.ds(at, row_count), :] = piece[1, :, cut].astype(jnp.float32)
    for j in range(tiles):
        f_s[j, pl.ds(pl.multiple_of(own + PAD, BLOCK), row_count), :] = own_start[:, j * LANES:(j + 1) * LANES]

    def forward(first_row, count, z_first, z_count):
        for k in range(3):
            for j in range(tiles):
                lhs_s[0:count, k * cells + j * LANES:k * cells + (j + 1) * LANES] = f_s[
                    j, pl.ds(PAD + first_row + (k - 1), count), :].astype(jnp.bfloat16)
        for n in range(cells // 256):
            value = dot(lhs_s[0:count, :], projector[:, n * 256:(n + 1) * 256])
            for part in range(2):
                t_s[2 * n + part, pl.ds(pl.multiple_of(PAD + first_row, BLOCK), count), :] = value[
                    :, part * LANES:(part + 1) * LANES]
        for w in range(tiles):
            a_s[w, pl.ds(pl.multiple_of(PAD + z_first, BLOCK), z_count), :] = t_s[
                w, pl.ds(PAD + z_first + offset_of(w), z_count), :]

    def transpose_part(n):
        columns = pl.ds(pl.multiple_of(n * 256, 256), 256)
        for k in range(3):
            rows = pl.ds(pl.multiple_of(k * cells + n * 256, 256), 256)
            for m in range(cells // 256):
                at = k * cells + m * 256
                across_s[rows, m * 256:(m + 1) * 256] = projector[at:at + 256, columns].T

    def adjoint(z_first, count):
        for k in range(3):
            for w in range(tiles):
                lhs_s[0:count, k * cells + w * LANES:k * cells + (w + 1) * LANES] = h_s[
                    w, pl.ds(PAD + z_first - offset_of(w) - (k - 1), count), :].astype(jnp.bfloat16)
        for n in range(cells // 256):
            value = dot(lhs_s[0:count, :], across_s[:, n * 256:(n + 1) * 256])
            for part in range(2):
                b_s[2 * n + part, pl.ds(pl.multiple_of(PAD + z_first, BLOCK), count), :] = value[
                    :, part * LANES:(part + 1) * LANES]

    def network(fields, plane, w1, w2, first_row, block_count, target, beside=None):
        count, shifted, _ = plane
        hidden_rows, depth = w1.shape
        out_rows = 2 * BLOCK * count
        group = len(x_refs[0])
        edge = jnp.zeros((out_rows, cells), jnp.float32)
        for slot in (LAG - 1, block_count + LAG):
            y_s[slot, 0:out_rows, :] = edge

        def build_taps(x, block):
            base = PAD + first_row + block * BLOCK
            mains = [[field[j, pl.ds(base, BLOCK), :] for j in range(tiles)] for field in fields]
            edges = []
            for j in range(tiles):
                value = jnp.zeros((BLOCK, LANES), jnp.float32)
                for c, field in enumerate(fields):
                    value = jnp.where(masks["rows"][2 * c], field[j, pl.ds(base - 1 - 2 * c, BLOCK), :], value)
                    value = jnp.where(masks["rows"][2 * c + 1], field[j, pl.ds(base + BLOCK - 1 - 2 * c, BLOCK), :], value)
                edges.append(value)
            moved = [shifted(main, masks) for main in mains]
            arrays = [each[s] for s in range(count) for each in moved] + shifted(edges, masks)
            if len(arrays) % 2:
                arrays.append([jnp.zeros((BLOCK, LANES), jnp.float32)] * tiles)
            for pair in range(len(arrays) // 2):
                for j in range(tiles):
                    x[pair * 16:(pair + 1) * 16, j * LANES:(j + 1) * LANES] = jnp.concatenate(
                        [arrays[2 * pair][j], arrays[2 * pair + 1][j]], axis=0).astype(jnp.bfloat16)

        def add_block(block):
            value = collapse(plane, block + LAG)
            inside = isinstance(block, int)
            base = PAD + first_row + (block if inside else jnp.maximum(block, 0)) * BLOCK
            for j in range(tiles):
                part = value[j] if inside else jnp.where(block >= 0, value[j], 0.0)
                target[j, pl.ds(base, BLOCK), :] += part

        def step(side, now, after, done):
            for u in range(max(len(now), len(after))):
                if u < len(now):
                    hidden = dot(w1[...], x_refs[side][u][0:depth, :]).astype(jnp.bfloat16)
                    hidden_refs[side][u][0:hidden_rows, :] = jnp.maximum(hidden, jnp.zeros_like(hidden))
                if u < len(after):
                    build_taps(x_refs[1 - side][u], after[u])
            for block in done:
                add_block(block)
            for u, block in enumerate(now):
                y_s[block + LAG, 0:out_rows, :] = dot(w2[...], hidden_refs[side][u][0:hidden_rows, :])

        def blocks_from(start):
            return [b for b in range(start, start + group) if 0 <= b < block_count]

        for u in range(group):
            build_taps(x_refs[0][u], u)
        per_turn = STEPS * group
        if block_count % per_turn == 0 and block_count > UNROLLED:
            @pl.loop(0, block_count // per_turn)
            def _(i):
                for phase in range(STEPS):
                    now = i * per_turn + phase * group
                    after = jnp.minimum(now + group, block_count - group)
                    step(phase % 2, [now + u for u in range(group)], [after + u for u in range(group)],
                         [now + u - group - 1 for u in range(group)])
                    if beside is not None and phase % 2 == 0:
                        beside(i * (STEPS // 2) + phase // 2)
        else:
            for turn in range(-(-block_count // group)):
                now = turn * group
                step(turn % 2, blocks_from(now), blocks_from(now + group), blocks_from(now - group - 1))
                if beside is not None and turn % 2 == 0:
                    beside(turn // 2)
        last = -(-block_count // group) * group
        for block in range(max(last - group - 1, 0), block_count):
            add_block(block)

    def collapse(plane, slot):
        def merged(s):
            at = s * 2 * BLOCK
            out = []
            for j in range(tiles):
                cut = slice(j * LANES, (j + 1) * LANES)
                outer = jnp.where(masks["rows"][0], y_s[slot - 1, at + BLOCK:at + 2 * BLOCK, cut], 0.0)
                outer = jnp.where(masks["rows"][BLOCK - 1], y_s[slot + 1, at + BLOCK:at + 2 * BLOCK, cut], outer)
                out.append(y_s[slot, at:at + BLOCK, cut] + outer)
            return out

        return plane[2](merged, masks)

    def reached(reach, unit=BLOCK):
        count = min(-(-(row_count + 2 * reach) // unit) * unit, total)
        return jnp.clip(own - (count - row_count) // 2, 0, total - count), count

    first, count = reached(3 * row_count + 7)
    forward(jnp.int32(-BLOCK), total + 2 * BLOCK, 0, total)
    quarters = cells // 256
    if count // (4 * BLOCK) == quarters:
        network((h_s, a_s, sino_s), DUAL, w1d, w2d, first, count // BLOCK, h_s, transpose_part)
    else:
        network((h_s, a_s, sino_s), DUAL, w1d, w2d, first, count // BLOCK, h_s)
        for n in range(quarters):
            transpose_part(n)
    first, count = reached(2 * row_count + 5, 2 * BLOCK)
    adjoint(first, count)
    network((f_s, b_s), PRIMAL, w1p, w2p, first, count // BLOCK, f_s)

    t_count = min(total + 2 * BLOCK, row_count + 10 * BLOCK)
    t_first = jnp.clip(own - 5 * BLOCK, -BLOCK, total + BLOCK - t_count)
    first, count = reached(row_count + 4, 2 * BLOCK)
    forward(t_first, t_count, first, count)
    first, count = reached(row_count + 3)
    network((h_s, a_s, sino_s), DUAL, w1d, w2d, first, count // BLOCK, h_s)
    first, count = reached(2, 2 * BLOCK)
    adjoint(first, count)
    first, count = reached(1)
    network((f_s, b_s), PRIMAL, w1p, w2p, first, count // BLOCK, f_s)
    for j in range(tiles):
        out[:, j * LANES:(j + 1) * LANES] = f_s[j, pl.ds(pl.multiple_of(own + PAD, BLOCK), row_count), :]


def gather(block, count):
    me = lax.axis_index("gz")
    window = min(count, 2 * HALO_BLOCKS + 1)
    if count & (count - 1) == 0 and count <= window:
        def swap(x, bits):
            return lax.ppermute(x, "gz", [(i, i ^ bits) for i in range(count)])

        held = {0: block}
        for bits in [2] * (count > 2) + list(range(count - 2, 3, -2)):
            held[bits] = swap(block, bits)
        if count > 1:
            for bits in list(held):
                held[bits ^ 1] = swap(held[bits], 1)
        return [held[b] for b in sorted(held)], [me ^ b for b in sorted(held)], me
    first = jnp.clip(me - HALO_BLOCKS, 0, count - window)
    whole = lax.all_gather(block, "gz", axis=0)
    return [whole[first + j] for j in range(window)], list(range(window)), me - first


def per_device(
    start_volume, sinogram, offsets, projector, dual_in, dual_out, primal_in, primal_out
):
    row_count, cells = start_volume.shape[1:]
    tiles = cells // LANES
    segment = lax.axis_index("segment")
    own_start = start_volume[segment]
    block = jnp.stack([own_start, sinogram[segment]]).astype(jnp.bfloat16)
    pieces, places, own = gather(block, lax.axis_size("gz"))
    window = len(pieces)
    total = window * row_count
    info = jnp.concatenate([
        jnp.stack([jnp.int32(own)] + [jnp.int32(p) for p in places]) * row_count,
        offsets[segment],
    ])
    dual_hidden, primal_hidden = dual_in.shape[0], primal_in.shape[0]
    parts = [dual_in.T, dual_out, primal_in.T, primal_out]
    packed = jnp.concatenate([
        jnp.pad(p, ((0, -p.shape[0] % 16), (0, primal_hidden - p.shape[1]))) for p in parts])
    blocks = total // BLOCK
    padded = total + 2 * PAD
    field = pltpu.VMEM((tiles, padded, LANES), jnp.float32)
    whole = pl.BlockSpec(memory_space=pltpu.VMEM)
    flat = projector.reshape(-1, cells)
    weights = pl.pallas_call(
        functools.partial(prepare, (dual_in.shape[::-1], primal_in.shape[::-1])),
        out_shape=[
            jax.ShapeDtypeStruct(shape, jnp.bfloat16) for shape in (
                (BLOCK * dual_hidden, 96), (48, BLOCK * dual_hidden),
                (BLOCK * primal_hidden, 224), (144, BLOCK * primal_hidden))
        ],
        in_specs=[whole],
        out_specs=[whole] * 4,
        cost_estimate=pl.CostEstimate(flops=2_000_000_000, bytes_accessed=8_000_000, transcendentals=0),
        compiler_params=pltpu.CompilerParams(vmem_limit_bytes=16 * 1024 * 1024),
        name="prepare",
    )(packed)
    operands = [own_start, *pieces, flat, *weights]
    result = pl.pallas_call(
        functools.partial(kernel, (window, tiles)),
        out_shape=jax.ShapeDtypeStruct((row_count, cells), jnp.float32),
        in_specs=[pl.BlockSpec(memory_space=pltpu.SMEM)] + [whole] * len(operands),
        out_specs=whole,
        scratch_shapes=[field] * 6 + [
            *[pltpu.VMEM((224, cells), jnp.bfloat16)] * 4,
            *[pltpu.VMEM((BLOCK * primal_hidden, cells), jnp.bfloat16)] * 4,
            pltpu.VMEM((min(blocks, 16) + LAG + 1, 144, cells), jnp.float32),
            pltpu.VMEM((total + 2 * BLOCK, 3 * cells), jnp.bfloat16),
            pltpu.VMEM((3 * cells, cells), jnp.bfloat16),
        ],
        compiler_params=pltpu.CompilerParams(vmem_limit_bytes=32 * 1024 * 1024),
        name="iterate",
    )(info, *operands)
    return result[None]


def solution(mesh):
    in_specs = (P(None, "gz", None), P(None, "gz", None), P(), P(), P(), P(), P(), P())
    out_specs = P("segment", "gz", None)
    return jax.shard_map(
        per_device, mesh=mesh, in_specs=in_specs, out_specs=out_specs, check_vma=False
    )
```

```python
import functools

import jax
import jax.numpy as jnp
import numpy as np
from jax import lax
from jax.experimental import pallas as pl
from jax.experimental.pallas import tpu as pltpu
from jax.sharding import PartitionSpec as P

IMG = 32
LANES = 128
BLOCK = 8
PAD = 16
HALO_BLOCKS = 5
LAG = 4
STEPS = 2
UNROLLED = 12


def dot(a, b):
    return jnp.dot(a, b, preferred_element_type=jnp.float32)


def lanes():
    return lax.broadcasted_iota(jnp.int32, (BLOCK, LANES), 1)


def rows_of():
    return lax.broadcasted_iota(jnp.int32, (BLOCK, LANES), 0)


def masks_of():
    lane = lanes()
    row = rows_of()
    column = lane % IMG
    return {
        "view": {-1: lane > 0, 1: lane < LANES - 1},
        "across": {-1: column > 0, 1: column < IMG - 1},
        "down": {-1: lane >= IMG, 1: lane < LANES - IMG},
        "rows": [row == r for r in range(BLOCK)],
    }


def shift_lanes(tiles, step, mask):
    return [jnp.where(mask, pltpu.roll(t, (-step) % LANES, 1), 0.0) for t in tiles]


def shift_down(tiles, dy, mask):
    rolled = [pltpu.roll(t, (-dy * IMG) % LANES, 1) for t in tiles]
    zero = jnp.zeros_like(tiles[0])
    beyond = rolled[1:] + [zero] if dy > 0 else [zero] + rolled[:-1]
    return [jnp.where(mask, near, far) for near, far in zip(rolled, beyond)]


def dual_shifted(tiles, masks):
    return [shift_lanes(tiles, -1, masks["view"][-1]), tiles, shift_lanes(tiles, 1, masks["view"][1])]


def dual_sum(values, masks):
    return add(add(shift_lanes(values(0), -1, masks["view"][-1]), values(1)),
               shift_lanes(values(2), 1, masks["view"][1]))


def primal_shifted(tiles, masks):
    across = [shift_lanes(tiles, -1, masks["across"][-1]), tiles, shift_lanes(tiles, 1, masks["across"][1])]
    return ([shift_down(t, -1, masks["down"][-1]) for t in across] + across
            + [shift_down(t, 1, masks["down"][1]) for t in across])


def primal_sum(values, masks):
    total = None
    for dy in (-1, 0, 1):
        at = (dy + 1) * 3
        part = add(add(shift_lanes(values(at), -1, masks["across"][-1]), values(at + 1)),
                   shift_lanes(values(at + 2), 1, masks["across"][1]))
        if dy:
            part = shift_down(part, dy, masks["down"][dy])
        total = part if total is None else add(total, part)
    return total


def add(a, b):
    return [x + y for x, y in zip(a, b)]


DUAL = (3, dual_shifted, dual_sum)
PRIMAL = (9, primal_shifted, primal_sum)


def iota(shape, dim):
    return lax.broadcasted_iota(jnp.int32, shape, dim)


def first_weights(w_in, taps, shift_count, channels, out):
    width = out.shape[1]
    hidden = w_in.shape[1]
    arrays = shift_count * channels
    main = arrays * BLOCK
    column = iota((taps, width), 1)
    row = iota((taps, width), 0)
    place = column - main
    outer = lax.bitwise_and(place, BLOCK - 1)
    outer_tap = (place // BLOCK) * channels + outer // 2
    used = (place >= 0) & (place < shift_count * BLOCK) & (outer < 2 * channels)
    low = used & (outer % 2 == 0)
    high = used & (outer % 2 == 1)
    for z in range(BLOCK):
        tap = (column % BLOCK - z + 1) * arrays + column // BLOCK
        hit = (place < 0) & (row == tap)
        if z == 0:
            hit = hit | (low & (row == outer_tap))
        if z == BLOCK - 1:
            hit = hit | (high & (row == outer_tap + 2 * arrays))
        table = jnp.where(hit, 1.0, 0.0).astype(jnp.bfloat16)
        out[z * hidden:(z + 1) * hidden, :] = lax.dot_general(
            w_in, table, (((0,), (0,)), ((), ())), preferred_element_type=jnp.float32
        ).astype(jnp.bfloat16)


def second_weights(w_out, hidden, shift_count, out):
    taps = w_out.shape[0]
    height, wide = out.shape
    spread = jnp.where(iota((hidden, wide), 1) % hidden == iota((hidden, wide), 0), 1.0, 0.0)
    across = dot(w_out, spread.astype(jnp.bfloat16)).astype(jnp.bfloat16)
    place = iota((height, taps), 0)
    tap = iota((height, taps), 1)
    shift = place // (2 * BLOCK)
    inner = (place // BLOCK) % 2 == 0
    row = place % BLOCK
    lane = iota((height, wide), 1) // hidden
    total = jnp.zeros((height, wide), jnp.float32)
    for z in range(BLOCK):
        hit = inner & (tap == (z + 1 - row) * shift_count + shift)
        if z == 0:
            hit = hit | (~inner & (row == BLOCK - 1) & (tap == 2 * shift_count + shift))
        if z == BLOCK - 1:
            hit = hit | (~inner & (row == 0) & (tap == shift))
        part = dot(jnp.where(hit, 1.0, 0.0).astype(jnp.bfloat16), across)
        total = jnp.where(lane == z, part, total)
    out[...] = total.astype(jnp.bfloat16)


def prepare(sizes, weights, w1d, w2d, w1p, w2p):
    (d_taps, d_hidden), (p_taps, p_hidden) = sizes
    at = 0
    parts = []
    for rows, columns in ((d_taps, d_hidden), (d_taps // 3, d_hidden), (p_taps, p_hidden),
                          (p_taps // 2, p_hidden)):
        parts.append(weights[at:at + rows, 0:columns])
        at += -(-rows // 16) * 16
    first_weights(parts[0], d_taps, 3, 3, w1d)
    second_weights(parts[1], d_hidden, 3, w2d)
    first_weights(parts[2], p_taps, 9, 2, w1p)
    second_weights(parts[3], p_hidden, 9, w2p)


def kernel(sizes, info, volumes, *refs):
    window, tiles = sizes
    pieces = refs[:window]
    (projector, w1d, w2d, w1p, w2p, out, f_s, sino_s, t_s, a_s, h_s, b_s,
     x_0, x_1, x_2, x_3, hidden_0, hidden_1, hidden_2, hidden_3, y_s, lhs_s,
     across_s, own_start, arrived) = refs[window:]
    x_refs, hidden_refs = ((x_0, x_1), (x_2, x_3)), ((hidden_0, hidden_1), (hidden_2, hidden_3))
    row_count = own_start.shape[0]
    own_copy = pltpu.make_async_copy(volumes.at[info[1 + window + tiles]], own_start, arrived)
    own_copy.start()
    total = window * row_count
    cells = tiles * LANES
    own = info[0]

    masks = masks_of()

    def offset_of(view):
        return info[1 + window + view]

    zero_rows = jnp.zeros((tiles, PAD, LANES), jnp.float32)
    for field in (f_s, sino_s, t_s, a_s):
        field[:, 0:PAD, :] = zero_rows
        field[:, PAD + total:PAD + total + PAD, :] = zero_rows
    h_s[...] = jnp.zeros(h_s.shape, jnp.float32)
    b_s[...] = jnp.zeros(b_s.shape, jnp.float32)
    for i, piece in enumerate(pieces):
        at = pl.multiple_of(info[1 + i] + PAD, BLOCK)
        for j in range(tiles):
            cut = slice(j * LANES, (j + 1) * LANES)
            f_s[j, pl.ds(at, row_count), :] = piece[0, :, cut].astype(jnp.float32)
            sino_s[j, pl.ds(at, row_count), :] = piece[1, :, cut].astype(jnp.float32)
    own_copy.wait()
    for j in range(tiles):
        f_s[j, pl.ds(pl.multiple_of(own + PAD, BLOCK), row_count), :] = own_start[:, j * LANES:(j + 1) * LANES]

    def forward(first_row, count, z_first, z_count):
        for k in range(3):
            for j in range(tiles):
                lhs_s[0:count, k * cells + j * LANES:k * cells + (j + 1) * LANES] = f_s[
                    j, pl.ds(PAD + first_row + (k - 1), count), :].astype(jnp.bfloat16)
        for n in range(cells // 256):
            value = dot(lhs_s[0:count, :], projector[:, n * 256:(n + 1) * 256])
            for part in range(2):
                t_s[2 * n + part, pl.ds(pl.multiple_of(PAD + first_row, BLOCK), count), :] = value[
                    :, part * LANES:(part + 1) * LANES]
        for w in range(tiles):
            a_s[w, pl.ds(pl.multiple_of(PAD + z_first, BLOCK), z_count), :] = t_s[
                w, pl.ds(PAD + z_first + offset_of(w), z_count), :]

    def transpose_part(n):
        columns = pl.ds(pl.multiple_of(n * 256, 256), 256)
        for k in range(3):
            rows = pl.ds(pl.multiple_of(k * cells + n * 256, 256), 256)
            for m in range(cells // 256):
                at = k * cells + m * 256
                across_s[rows, m * 256:(m + 1) * 256] = projector[at:at + 256, columns].T

    def adjoint(z_first, count):
        for k in range(3):
            for w in range(tiles):
                lhs_s[0:count, k * cells + w * LANES:k * cells + (w + 1) * LANES] = h_s[
                    w, pl.ds(PAD + z_first - offset_of(w) - (k - 1), count), :].astype(jnp.bfloat16)
        for n in range(cells // 256):
            value = dot(lhs_s[0:count, :], across_s[:, n * 256:(n + 1) * 256])
            for part in range(2):
                b_s[2 * n + part, pl.ds(pl.multiple_of(PAD + z_first, BLOCK), count), :] = value[
                    :, part * LANES:(part + 1) * LANES]

    def network(fields, plane, w1, w2, first_row, block_count, target, beside=None):
        count, shifted, _ = plane
        hidden_rows, depth = w1.shape
        out_rows = 2 * BLOCK * count
        group = len(x_refs[0])
        edge = jnp.zeros((out_rows, cells), jnp.float32)
        for slot in (LAG - 1, block_count + LAG):
            y_s[slot, 0:out_rows, :] = edge

        def build_taps(x, block):
            base = PAD + first_row + block * BLOCK
            mains = [[field[j, pl.ds(base, BLOCK), :] for j in range(tiles)] for field in fields]
            edges = []
            for j in range(tiles):
                value = jnp.zeros((BLOCK, LANES), jnp.float32)
                for c, field in enumerate(fields):
                    value = jnp.where(masks["rows"][2 * c], field[j, pl.ds(base - 1 - 2 * c, BLOCK), :], value)
                    value = jnp.where(masks["rows"][2 * c + 1], field[j, pl.ds(base + BLOCK - 1 - 2 * c, BLOCK), :], value)
                edges.append(value)
            moved = [shifted(main, masks) for main in mains]
            arrays = [each[s] for s in range(count) for each in moved] + shifted(edges, masks)
            if len(arrays) % 2:
                arrays.append([jnp.zeros((BLOCK, LANES), jnp.float32)] * tiles)
            for pair in range(len(arrays) // 2):
                for j in range(tiles):
                    x[pair * 16:(pair + 1) * 16, j * LANES:(j + 1) * LANES] = jnp.concatenate(
                        [arrays[2 * pair][j], arrays[2 * pair + 1][j]], axis=0).astype(jnp.bfloat16)

        def add_block(block):
            value = collapse(plane, block + LAG)
            inside = isinstance(block, int)
            base = PAD + first_row + (block if inside else jnp.maximum(block, 0)) * BLOCK
            for j in range(tiles):
                part = value[j] if inside else jnp.where(block >= 0, value[j], 0.0)
                target[j, pl.ds(base, BLOCK), :] += part

        def step(side, now, after, done):
            for u in range(max(len(now), len(after))):
                if u < len(now):
                    hidden = dot(w1[...], x_refs[side][u][0:depth, :]).astype(jnp.bfloat16)
                    hidden_refs[side][u][0:hidden_rows, :] = jnp.maximum(hidden, jnp.zeros_like(hidden))
                if u < len(after):
                    build_taps(x_refs[1 - side][u], after[u])
            for block in done:
                add_block(block)
            for u, block in enumerate(now):
                y_s[block + LAG, 0:out_rows, :] = dot(w2[...], hidden_refs[side][u][0:hidden_rows, :])

        def blocks_from(start):
            return [b for b in range(start, start + group) if 0 <= b < block_count]

        for u in range(group):
            build_taps(x_refs[0][u], u)
        per_turn = STEPS * group
        if block_count % per_turn == 0 and block_count > UNROLLED:
            @pl.loop(0, block_count // per_turn)
            def _(i):
                for phase in range(STEPS):
                    now = i * per_turn + phase * group
                    after = jnp.minimum(now + group, block_count - group)
                    step(phase % 2, [now + u for u in range(group)], [after + u for u in range(group)],
                         [now + u - group - 1 for u in range(group)])
                    if beside is not None and phase % 2 == 0:
                        beside(i * (STEPS // 2) + phase // 2)
        else:
            for turn in range(-(-block_count // group)):
                now = turn * group
                step(turn % 2, blocks_from(now), blocks_from(now + group), blocks_from(now - group - 1))
                if beside is not None and turn % 2 == 0:
                    beside(turn // 2)
        last = -(-block_count // group) * group
        for block in range(max(last - group - 1, 0), block_count):
            add_block(block)

    def collapse(plane, slot):
        def merged(s):
            at = s * 2 * BLOCK
            out = []
            for j in range(tiles):
                cut = slice(j * LANES, (j + 1) * LANES)
                outer = jnp.where(masks["rows"][0], y_s[slot - 1, at + BLOCK:at + 2 * BLOCK, cut], 0.0)
                outer = jnp.where(masks["rows"][BLOCK - 1], y_s[slot + 1, at + BLOCK:at + 2 * BLOCK, cut], outer)
                out.append(y_s[slot, at:at + BLOCK, cut] + outer)
            return out

        return plane[2](merged, masks)

    def reached(reach, unit=BLOCK):
        count = min(-(-(row_count + 2 * reach) // unit) * unit, total)
        return jnp.clip(own - (count - row_count) // 2, 0, total - count), count

    first, count = reached(3 * row_count + 7)
    forward(jnp.int32(-BLOCK), total + 2 * BLOCK, 0, total)
    quarters = cells // 256
    if count // (4 * BLOCK) == quarters:
        network((h_s, a_s, sino_s), DUAL, w1d, w2d, first, count // BLOCK, h_s, transpose_part)
    else:
        network((h_s, a_s, sino_s), DUAL, w1d, w2d, first, count // BLOCK, h_s)
        for n in range(quarters):
            transpose_part(n)
    first, count = reached(2 * row_count + 5, 2 * BLOCK)
    adjoint(first, count)
    network((f_s, b_s), PRIMAL, w1p, w2p, first, count // BLOCK, f_s)

    t_count = min(total + 2 * BLOCK, row_count + 10 * BLOCK)
    t_first = jnp.clip(own - 5 * BLOCK, -BLOCK, total + BLOCK - t_count)
    first, count = reached(row_count + 4, 2 * BLOCK)
    forward(t_first, t_count, first, count)
    first, count = reached(row_count + 3)
    network((h_s, a_s, sino_s), DUAL, w1d, w2d, first, count // BLOCK, h_s)
    first, count = reached(2, 2 * BLOCK)
    adjoint(first, count)
    first, count = reached(1)
    network((f_s, b_s), PRIMAL, w1p, w2p, first, count // BLOCK, f_s)
    for j in range(tiles):
        out[:, j * LANES:(j + 1) * LANES] = f_s[j, pl.ds(pl.multiple_of(own + PAD, BLOCK), row_count), :]


def gather(block, count):
    me = lax.axis_index("gz")
    window = min(count, 2 * HALO_BLOCKS + 1)
    if count & (count - 1) == 0 and count <= window:
        def swap(x, bits):
            return lax.ppermute(x, "gz", [(i, i ^ bits) for i in range(count)])

        held = {0: block}
        for bits in [2] * (count > 2) + list(range(count - 2, 3, -2)):
            held[bits] = swap(block, bits)
        if count > 1:
            for bits in list(held):
                held[bits ^ 1] = swap(held[bits], 1)
        return [held[b] for b in sorted(held)], [me ^ b for b in sorted(held)], me
    first = jnp.clip(me - HALO_BLOCKS, 0, count - window)
    whole = lax.all_gather(block, "gz", axis=0)
    return [whole[first + j] for j in range(window)], list(range(window)), me - first


def per_device(
    start_volume, sinogram, offsets, projector, dual_in, dual_out, primal_in, primal_out
):
    row_count, cells = start_volume.shape[1:]
    tiles = cells // LANES
    segment = lax.axis_index("segment")
    own_start = start_volume[segment]
    block = jnp.stack([own_start, sinogram[segment]]).astype(jnp.bfloat16)
    pieces, places, own = gather(block, lax.axis_size("gz"))
    window = len(pieces)
    total = window * row_count
    info = jnp.concatenate([
        jnp.stack([jnp.int32(own)] + [jnp.int32(p) for p in places]) * row_count,
        offsets[segment],
        segment.astype(jnp.int32)[None],
    ])
    dual_hidden, primal_hidden = dual_in.shape[0], primal_in.shape[0]
    parts = [dual_in.T, dual_out, primal_in.T, primal_out]
    packed = jnp.concatenate([
        jnp.pad(p, ((0, -p.shape[0] % 16), (0, primal_hidden - p.shape[1]))) for p in parts])
    blocks = total // BLOCK
    padded = total + 2 * PAD
    field = pltpu.VMEM((tiles, padded, LANES), jnp.float32)
    whole = pl.BlockSpec(memory_space=pltpu.VMEM)
    flat = projector.reshape(-1, cells)
    weights = pl.pallas_call(
        functools.partial(prepare, (dual_in.shape[::-1], primal_in.shape[::-1])),
        out_shape=[
            jax.ShapeDtypeStruct(shape, jnp.bfloat16) for shape in (
                (BLOCK * dual_hidden, 96), (48, BLOCK * dual_hidden),
                (BLOCK * primal_hidden, 224), (144, BLOCK * primal_hidden))
        ],
        in_specs=[whole],
        out_specs=[whole] * 4,
        cost_estimate=pl.CostEstimate(flops=2_000_000_000, bytes_accessed=8_000_000, transcendentals=0),
        compiler_params=pltpu.CompilerParams(vmem_limit_bytes=16 * 1024 * 1024),
        name="prepare",
    )(packed)
    operands = [start_volume, *pieces, flat, *weights]
    result = pl.pallas_call(
        functools.partial(kernel, (window, tiles)),
        out_shape=jax.ShapeDtypeStruct((row_count, cells), jnp.float32),
        in_specs=[pl.BlockSpec(memory_space=pltpu.SMEM), pl.BlockSpec(memory_space=pl.ANY)]
        + [whole] * (len(operands) - 1),
        out_specs=whole,
        scratch_shapes=[field] * 6 + [
            *[pltpu.VMEM((224, cells), jnp.bfloat16)] * 4,
            *[pltpu.VMEM((BLOCK * primal_hidden, cells), jnp.bfloat16)] * 4,
            pltpu.VMEM((min(blocks, 16) + LAG + 1, 144, cells), jnp.float32),
            pltpu.VMEM((total + 2 * BLOCK, 3 * cells), jnp.bfloat16),
            pltpu.VMEM((3 * cells, cells), jnp.bfloat16),
            pltpu.VMEM((row_count, cells), jnp.float32),
            pltpu.SemaphoreType.DMA,
        ],
        compiler_params=pltpu.CompilerParams(vmem_limit_bytes=32 * 1024 * 1024),
        name="iterate",
    )(info, *operands)
    return result[None]


def solution(mesh):
    in_specs = (P(None, "gz", None), P(None, "gz", None), P(), P(), P(), P(), P(), P())
    out_specs = P("segment", "gz", None)
    return jax.shard_map(
        per_device, mesh=mesh, in_specs=in_specs, out_specs=out_specs, check_vma=False
    )
```
